32 devices in a mesh: pulse: 2 (over y), grid: 16 (over z, x, core).
Axes of the slice: x: 2, y: 2, z: 4, core: 2. Of those that a mesh axis runs over, the one named last changes fastest.
Arguments:
- orbitals: float32 [16, 32, 32, 256], P('grid'), may hold values from -6 to 6
- potential: float32 [16, 32, 32], P('grid'), may hold values from -2 to 2
- pulse: float32 [2], P('pulse'), parts along dimension 0, may hold values from -3 to 3
- projectors: bfloat16 [256, 8, 256], P('grid'), may hold values from -0.375 to 0.375
- couplings: float32 [256, 8], P('grid'), may hold values from 1 to 8
- sphere_points: int32 [256, 256], P('grid'), may hold values from 0 to 1023
- atom_count: int32 [16], P('grid'), may hold values from 1 to 16, as said below
Outputs:
- propagated: float32 [32, 32, 32, 256], P(('pulse', 'grid')), parts along dimension 0
- dipole: float32 [2], P('pulse'), parts along dimension 0
The draws below stay inside these ranges and needn't reach their ends.
There are 2 independent parts, one for each index of `pulse`. The reference program is written for one: setup_inputs(seed, part) draws one part's arguments, and reference() takes and returns one part's arrays. A program takes and returns all parts, laid end to end along the dimension named above; an argument that names none is the same for every part. Nothing has to cross between parts.
Inputs may be any that keep to these rules, and one draw needn't show every extreme that they name: The first and last slab are full: atom_count of them is 16. Slabs within an eighth of the axis from either end hold three quarters or more of 16 atoms, the others at most a quarter.
All inputs are finite; a program needn't handle non-finite values.
Results may differ from the reference program's by a relative error of at most 0.0003.
Values sent between devices are 32-bit elements; how exact they have to be, the bound alone decides.
No kernel may reach another device: no remote copies, remote signals or barrier semaphores. Data moves between devices by JAX's collectives and lax.ppermute only.
A program may use at most 64 MiB of HBM per device.

```python
import math
import jax
import jax.numpy as jnp
from jax import lax

CZ = 1
NX = 32
NY = 32
NB = 128
ATOM_DEV = 16
K = 8
P_SIZE = 256
TERMS = 4
NZ = 16
SLABS = 16
ATOMS = 256


def draw_atom_count(key, part):
    key = jax.random.fold_in(key, 7)
    key_high, key_low = jax.random.split(key)
    edge_slabs = max(SLABS // 8, 1)
    position = jnp.arange(SLABS)
    crowded = (position < edge_slabs) | (position >= SLABS - edge_slabs)
    high_counts = jax.random.randint(key_high, (SLABS,), ATOM_DEV * 3 // 4, ATOM_DEV + 1)
    low_counts = jax.random.randint(key_low, (SLABS,), 1, ATOM_DEV // 4 + 1)
    counted = jnp.where(crowded, high_counts, low_counts)
    counted = counted.at[0].set(ATOM_DEV).at[SLABS - 1].set(ATOM_DEV)
    return counted.astype(jnp.int32)


def set_ends(entries, key, smallest, high):
    dims = entries.shape
    index_at = [jax.random.randint(jax.random.fold_in(key, axis), (), 0, dims[axis]) for axis in range(len(dims))]
    entries = entries.at[tuple(index_at)].set(smallest)
    longest = dims.index(max(dims))
    index_at[longest] = (index_at[longest] + 1) % dims[longest]
    return entries.at[tuple(index_at)].set(high)


def block_levels(own_key, shape, shards, low, high):
    factor_of = 1.0
    for dim, parts in shards:
        heights = jax.random.uniform(jax.random.fold_in(jax.random.fold_in(own_key, 6), dim), (parts,), jnp.float32, low / len(shards), high / len(shards))
        factor_of = factor_of * jnp.repeat(jnp.exp(heights), shape[dim] // parts).reshape((-1,) + (1,) * (len(shape) - 1 - dim))
    return factor_of


def normal_values(own_key, shape, width, most, shards=(), kind=jnp.bfloat16):
    loudness = block_levels(own_key, shape, shards, -0.22, 0.18) if shards else 1.0
    drawn = jax.random.normal(own_key, shape, jnp.float32) * width * loudness
    return jnp.minimum(jnp.maximum(drawn, -most), most).astype(kind)


def setup_inputs(seed: int = 0, part: int = 0) -> dict:
    key_list = jax.random.split(jax.random.key(seed), 8)
    part_keys = jax.random.split(jax.random.fold_in(key_list[7], part), 8)
    orbitals = normal_values(key_list[0], (NZ, NX, NY, 2 * NB), 1.0, 6.0, ((0, 16),), jnp.float32)
    potential = jnp.clip(jax.random.uniform(key_list[1], (NZ, NX, NY), jnp.float32, -2.0, 2.0) * block_levels(key_list[1], (NZ, NX, NY), ((0, 16),), -0.4, 0.0), -2.0, 2.0)
    pulse = normal_values(part_keys[2], (1,), 1.0, 3.0, (), jnp.float32)
    projectors = normal_values(key_list[3], (ATOMS, K, P_SIZE), P_SIZE ** -0.5, 0.375, ((0, 16),))
    couplings = jnp.clip(jnp.exp(math.log(8.0) - 2.0794415 * jax.random.uniform(key_list[4], (ATOMS, K), jnp.float32) ** block_levels(key_list[4], (ATOMS, K), ((0, 16),), -0.2, 0.2)), 1.0, 8.0)
    sphere_points = set_ends(jax.random.randint(key_list[5], (ATOMS, P_SIZE), 0, CZ * NX * NY), jax.random.fold_in(key_list[5], 1), 0, (CZ * NX * NY) - 1).astype(jnp.int32)
    atom_count = draw_atom_count(jax.random.fold_in(key_list[7], 71), part)
    return dict(orbitals=orbitals, potential=potential, pulse=pulse, projectors=projectors, couplings=couplings, sphere_points=sphere_points, atom_count=atom_count)


time_step = 0.1


def hamiltonian(field, potential, applied, projectors, couplings, sphere_points, atom_count):
    padded = jnp.pad(field, ((1, 1), (0, 0), (0, 0), (0, 0)))
    laplace = padded[2:] + padded[:-2]
    laplace = laplace + jnp.roll(field, 1, 1) + jnp.roll(field, -1, 1)
    laplace = laplace + jnp.roll(field, 1, 2) + jnp.roll(field, -1, 2) - 6.0 * field
    local_part = -0.5 * laplace + (potential + applied)[..., None] * field
    channels = field.shape[3]
    flat_field = field.reshape(-1, channels)
    slab_cells = CZ * NX * NY
    proj_slabs = projectors.astype(jnp.float32).reshape(SLABS, ATOM_DEV, K, P_SIZE)
    coup_slabs = couplings.reshape(SLABS, ATOM_DEV, K)
    point_slabs = sphere_points.reshape(SLABS, ATOM_DEV, P_SIZE)
    offsets = (jnp.arange(SLABS) * slab_cells).astype(jnp.int32)

    def one_slab(target, inputs):
        proj_slab, coup_slab, point_slab, counted, offset = inputs
        global_points = point_slab + offset
        samples = flat_field[global_points]
        coeffs = jnp.einsum("akp,apc->akc", proj_slab, samples, precision=lax.Precision.HIGHEST)
        occupied = (jnp.arange(ATOM_DEV) < counted).astype(jnp.float32)
        weights = coup_slab * occupied[:, None]
        scaled = coeffs * weights[:, :, None]
        contribution = jnp.einsum("akp,akc->apc", proj_slab, scaled, precision=lax.Precision.HIGHEST)
        target = target.at[global_points.reshape(-1)].add(contribution.reshape(-1, channels))
        return target, None

    flat_out, unused = lax.scan(one_slab, local_part.reshape(-1, channels),
                                (proj_slabs, coup_slabs, point_slabs, atom_count, offsets))
    return flat_out.reshape(field.shape)


def reference(orbitals, potential, pulse, projectors, couplings, sphere_points, atom_count):
    planes = (jnp.arange(NZ).astype(jnp.float32) + 0.5) / NZ
    applied = (pulse[0] * 4.0 * (planes - 0.5))[:, None, None]
    series_term = orbitals
    summed = orbitals
    for order in range(1, TERMS + 1):
        image = hamiltonian(series_term, potential, applied, projectors, couplings, sphere_points, atom_count)
        factor = time_step / order
        series_term = jnp.concatenate([factor * image[..., NB:], -factor * image[..., :NB]], axis=3)
        summed = summed + series_term
    moment = jnp.sum(planes[:, None, None, None] * summed * summed)
    dipole = moment / (NZ * NX * NY * NB)
    return summed, dipole.reshape(1)
```

```python
import functools

import jax
import jax.numpy as jnp
from jax import lax
from jax.experimental import pallas as pl
from jax.experimental.pallas import tpu as pltpu
from jax.sharding import PartitionSpec as P


TERMS = 4
TIME_STEP = 0.1
GROUP = 4
HALO = TERMS
SLOTS = GROUP + 2 * HALO
LIGHT = 4
F32 = jnp.float32
BF16 = jnp.bfloat16
NT = (((1,), (1,)), ((), ()))
NN = (((1,), (0,)), ((), ()))


def iota(shape, dim):
    return lax.broadcasted_iota(jnp.int32, shape, dim)


def split(value):
    high = value.astype(BF16)
    return high, (value - high.astype(F32)).astype(BF16)


def place():
    y, g = lax.axis_index("pulse"), lax.axis_index("grid")
    return y, g // GROUP, (g // 2) % 2, g % 2


def pack_kernel(orb, pot, proj, coup, points, count, near, far, heavy, packed, rows):
    y, _, x, _ = place()
    cells, channels = orb.shape
    lanes = cells // 8
    half = channels // 2
    first = iota((lanes, half), 1) < half // 2
    for j in range(8):
        chunk = slice(j * lanes, (j + 1) * lanes)
        re, im = orb[chunk, :half], orb[chunk, half:]
        low = jnp.where(first, re, pltpu.roll(im, half // 2, 1))
        high = jnp.where(first, pltpu.roll(re, half // 2, 1), im)
        packed[chunk, :] = jnp.where(y == 0, low, high)
    for j in range(8):
        rows[:, j * lanes : (j + 1) * lanes] = packed[pl.ds(j, lanes, stride=8), :].T
    part = half // 8
    for out, xx in ((near, x), (far, 1 - x)):
        for c in range(2):
            start = pl.multiple_of((2 * xx + c) * part, part)
            out[c * 2 * part : c * 2 * part + part, :] = rows[pl.ds(start, part), :]
            out[c * 2 * part + part : (c + 1) * 2 * part, :] = rows[pl.ds(start + half // 2, part), :]
    nx, ny = pot.shape
    yh = ny // 8
    col = iota((ny, cells), 1)
    pick = (iota((ny, cells), 0) == (col % lanes) % yh * 8 + col // lanes).astype(F32)
    spread = lax.dot_general(pot[...], pick, NN, precision=lax.Precision.HIGHEST, preferred_element_type=F32)
    keep = iota((nx, cells), 0) == (iota((nx, cells), 1) % lanes) // yh
    pot_row = jnp.sum(jnp.where(keep, spread, 0.0), axis=0, keepdims=True)
    atoms, k = coup.shape
    pick = (iota((k, atoms * k), 0) == iota((k, atoms * k), 1) % k).astype(F32)
    spread = lax.dot_general(coup[...], pick, NN, precision=lax.Precision.HIGHEST, preferred_element_type=F32)
    atom = iota((atoms, atoms * k), 0)
    keep = (atom == iota((atoms, atoms * k), 1) // k) & (atom < count[0])
    weight_row = jnp.sum(jnp.where(keep, spread, 0.0), axis=0, keepdims=True)
    size = points.shape[1]
    base = 4 * part
    for out in (near, far):
        for a in range(LIGHT):
            out[base : base + k, a * size : (a + 1) * size] = proj[a].astype(F32)
            out[base + k : base + k + 1, a * size : (a + 1) * size] = points[a : a + 1, :].astype(F32)
        out[base + k + 1 : base + k + 2, :] = pot_row
        out[base + k + 2 : base + k + 3, :] = jnp.zeros((1, cells), F32)
        out[base + k + 2 : base + k + 3, : atoms * k] = weight_row
        out[base + k + 3 : base + k + 8, :] = jnp.zeros((5, cells), F32)
    groups = atoms // LIGHT - 1
    for group in range(groups):
        for a in range(LIGHT):
            source = (group + 1) * LIGHT + a
            heavy[group * k : (group + 1) * k, a * size : (a + 1) * size] = proj[source].astype(F32)
            heavy[groups * k + group : groups * k + group + 1, a * size : (a + 1) * size] = (
                points[source : source + 1, :].astype(F32)
            )
    heavy[groups * (k + 1) :, :] = jnp.zeros((heavy.shape[0] - groups * (k + 1), cells), F32)


def matrix_of(proj, points, size):
    k = proj.shape[0]
    parts = []
    for a in range(LIGHT):
        values = proj[:, a * size : (a + 1) * size]
        cell = points[:, a * size : (a + 1) * size].astype(jnp.int32)
        low, lane = cell & 7, cell >> 3
        tall = jnp.concatenate([jnp.where(low == j, values, 0.0) for j in range(8)], axis=0).astype(BF16)
        hot = jnp.where(iota((128, size), 0) == lane, 1.0, 0.0).astype(BF16)
        sums = lax.dot_general(tall, hot, NT, preferred_element_type=F32)
        parts.append(jnp.concatenate([sums[j * k : (j + 1) * k, :] for j in range(8)], axis=1))
    return jnp.concatenate(parts, axis=0)


def roll_lanes(value, shift):
    return pltpu.roll(value, shift % value.shape[1], 1)


def evolve_kernel(slabs, shared_heavy, *refs):
    own_pulse, other_pulse = refs[:2]
    bundles = refs[2:14]
    heavies = refs[14:16] if not shared_heavy else refs[14:15]
    refs = refs[14 + len(heavies) :]
    outs, moment = refs[:4], refs[4]
    start, ping, pong, start_split, term_split, total, light, full, pots, weights, nonlocal_part = refs[5:]
    y, quad, x, c = place()
    quads = slabs // GROUP
    part = start.shape[1] // 2
    cells = start.shape[2]
    k = 8
    size = cells // LIGHT
    base = 4 * part
    span = LIGHT * k
    edge = max(slabs // 8, 1)
    has_low, has_high = quad > 0, quad < quads - 1

    for number, bundle in enumerate(bundles):
        direction, xf, cf = number // 4, number // 2 % 2, number % 2
        slot = direction * GROUP + 2 * (x if xf == 0 else 1 - x) + (c if cf == 0 else 1 - c)
        rows = bundle[pl.ds(pl.multiple_of(c * 2 * part, 2 * part), 2 * part), :]
        start[slot] = rows
        high, low = split(rows)
        start_split[slot, : 2 * part] = high
        start_split[slot, 2 * part :] = low
        pots[slot] = bundle[base + k + 1 : base + k + 2, :]
        weights[slot] = bundle[base + k + 2 : base + k + 3, : 4 * span]

        def build(bundle=bundle, slot=slot):
            matrix = matrix_of(bundle[base : base + k, :], bundle[base + k : base + k + 1, :], size)
            high, low = split(matrix)
            light[slot, :span] = high
            light[slot, span : 2 * span] = low
            light[slot, 2 * span :] = high

        if direction == 1:
            build()
        else:
            pl.when((has_low if direction == 0 else has_high) & (slot > 0) & (slot < SLOTS - 1))(build)

    def plane_of(slot):
        return quad * GROUP + slot - HALO

    def is_heavy(slot):
        plane = plane_of(slot)
        return (plane < edge) | (plane >= slabs - edge)

    def build_full(store, source, slot):
        wide = 4 * span
        full[store, 0:span] = light[slot, :span]
        full[store, wide : wide + span] = light[slot, span : 2 * span]
        full[store, 2 * wide : 2 * wide + span] = light[slot, :span]
        for group in range(3):
            high, low = split(
                matrix_of(source(group * k, k), source(3 * k + group, 1), size)
            )
            at = (group + 1) * span
            full[store, at : at + span] = high
            full[store, wide + at : wide + at + span] = low
            full[store, 2 * wide + at : 2 * wide + at + span] = high

    if shared_heavy:

        def store_of(slot):
            return slot - 1

        for slot in range(1, SLOTS - 1):
            exists = (plane_of(slot) >= 0) & (plane_of(slot) < slabs)

            @pl.when(exists & is_heavy(slot))
            def _(slot=slot):
                build_full(slot - 1, lambda at, n: heavies[0][slot - 1, at : at + n, :], slot)
    else:
        ends = (quad == 0) | (quad == quads - 1)
        beside = (quad == 1) | (quad == quads - 2)
        low_end = quad <= 1
        first_slot = jnp.where(ends, jnp.where(low_end, HALO, HALO + 2), jnp.where(low_end, 1, SLOTS - 2))

        def store_of(slot):
            return jnp.where(ends, slot - first_slot, 0)

        @pl.when(ends)
        def _():
            for cf in range(2):
                core = c if cf == 0 else 1 - c
                build_full(core, lambda at, n, cf=cf: heavies[cf][at : at + n, :], first_slot + core)

        @pl.when(beside)
        def _():
            mine = (c == 1) == low_end

            def source(at, n):
                return jnp.where(mine, heavies[0][at : at + n, :], heavies[1][at : at + n, :])

            build_full(0, source, first_slot)

    @pl.when(jnp.logical_not(has_low))
    def _():
        ping[HALO - 1] = jnp.zeros(ping.shape[1:], F32)
        pong[HALO - 1] = jnp.zeros(pong.shape[1:], F32)

    @pl.when(jnp.logical_not(has_high))
    def _():
        ping[HALO + GROUP] = jnp.zeros(ping.shape[1:], F32)
        pong[HALO + GROUP] = jnp.zeros(pong.shape[1:], F32)

    def project(halves, slot, count):
        def run(matrix, width):
            r = lax.dot_general(halves, matrix(0, 2 * width), NT, preferred_element_type=F32)
            coeffs = r[:count, :width] + r[count:, :width] + r[:count, width:]
            scaled = coeffs * weights[slot][:, :width]
            high, low = split(scaled)
            wide = jnp.concatenate([high, high, low], axis=1)
            nonlocal_part[:count] = lax.dot_general(wide, matrix(0, 3 * width), NN, preferred_element_type=F32)

        heavy = is_heavy(slot)

        @pl.when(heavy)
        def _():
            store = store_of(slot)
            run(lambda a, n: full[store, a : a + n, :], 4 * span)

        @pl.when(jnp.logical_not(heavy))
        def _():
            run(lambda a, n: light[slot, a : a + n, :], span)

    lane = iota((1, 128), 1)
    groups_y = 4
    wrap_up, wrap_down = lane % groups_y == groups_y - 1, lane % groups_y == 0

    def hamiltonian(field, slot, j, shift):
        cols = slice(j * 128, (j + 1) * 128)
        v = field[slot, :, cols]
        around = field[slot - 1, :, cols] + field[slot + 1, :, cols]
        around += roll_lanes(v, groups_y) + roll_lanes(v, -groups_y)
        if j < 7:
            around += field[slot, :, (j + 1) * 128 : (j + 2) * 128]
        else:
            w = field[slot, :, :128]
            around += jnp.where(wrap_up, roll_lanes(w, groups_y - 1), roll_lanes(w, -1))
        if j > 0:
            around += field[slot, :, (j - 1) * 128 : j * 128]
        else:
            w = field[slot, :, 7 * 128 :]
            around += jnp.where(wrap_down, roll_lanes(w, 1 - groups_y), roll_lanes(w, 1))
        return (pots[slot][:, cols] + shift) * v - 0.5 * around + nonlocal_part[: v.shape[0], cols], v

    def pulse_field(slot, p):
        strength = jnp.where(y == p, own_pulse[0], other_pulse[0])
        position = (plane_of(slot).astype(F32) + 0.5) / slabs
        return strength * 4.0 * (position - 0.5)

    def put(target, slot, rows, cols, value):
        target[slot, rows, cols] = value
        high, low = split(value)
        term_split[slot, rows, cols] = high
        term_split[slot, slice(4 * part + rows.start, 4 * part + rows.stop), cols] = low

    def bounds(order):
        reach = TERMS - order
        low = jnp.where(has_low, HALO - reach, HALO)
        high = jnp.where(has_high, HALO + GROUP + reach, HALO + GROUP)
        return low, high

    def first(slot, carry):
        project(start_split[slot], slot, 2 * part)
        fields = [pulse_field(slot, p) for p in range(2)]
        own = (slot >= HALO) & (slot < HALO + GROUP)
        for j in range(8):
            cols = slice(j * 128, (j + 1) * 128)
            h, v = hamiltonian(start, slot, j, 3.0)
            for p in range(2):
                image = h + fields[p] * v
                put(ping, slot, slice(p * part, (p + 1) * part), cols, TIME_STEP * image[part:])
                put(ping, slot, slice((2 + p) * part, (3 + p) * part), cols, -TIME_STEP * image[:part])

        @pl.when(own)
        def _():
            for p in range(2):
                for ri in range(2):
                    rows = slice((2 * ri + p) * part, (2 * ri + p + 1) * part)
                    total[slot - HALO, rows] = start[slot, ri * part : (ri + 1) * part] + ping[slot, rows]

        return carry

    lax.fori_loop(*bounds(1), first, 0)

    def later(order, source, target):
        factor = TIME_STEP / order

        def run(slot, carry):
            project(term_split[slot], slot, 4 * part)
            fields = [pulse_field(slot, p) for p in range(2)]
            pulse_of_row = iota((4 * part, 1), 0) // part % 2
            shift = jnp.where(pulse_of_row == 0, 3.0 + fields[0], 3.0 + fields[1])
            own = (slot >= HALO) & (slot < HALO + GROUP)
            index = jnp.clip(slot - HALO, 0, GROUP - 1)
            for j in range(8):
                cols = slice(j * 128, (j + 1) * 128)
                image, _ = hamiltonian(source, slot, j, shift)
                re, im = factor * image[2 * part :], -factor * image[: 2 * part]
                if order < TERMS:
                    put(target, slot, slice(0, 2 * part), cols, re)
                    put(target, slot, slice(2 * part, 4 * part), cols, im)

                    @pl.when(own)
                    def _(re=re, im=im, cols=cols):
                        total[index, : 2 * part, cols] += re
                        total[index, 2 * part :, cols] += im
                else:
                    total[index, : 2 * part, cols] += re
                    total[index, 2 * part :, cols] += im
            return carry

        lax.fori_loop(*bounds(order), run, 0)

    later(2, ping, pong)
    later(3, pong, ping)
    later(4, ping, pong)

    for p in range(2):
        value = jnp.zeros((part, 128), F32)
        for slot in range(GROUP):
            position = (plane_of(slot + HALO).astype(F32) + 0.5) / slabs
            squares = jnp.zeros((part, 128), F32)
            for ri in range(2):
                for j in range(8):
                    v = total[slot, (2 * ri + p) * part : (2 * ri + p + 1) * part, j * 128 : (j + 1) * 128]
                    squares += v * v
            value += position * squares
        moment[p : p + 1, :] = jnp.full((1, 128), jnp.sum(value), F32)
    for number, out in enumerate(outs):
        yy = y if number // 2 == 0 else 1 - y
        xx = x if number % 2 == 0 else 1 - x
        for core in range(2):
            for ri in range(2):
                start_row = pl.multiple_of((2 * ri + yy) * part, part)
                at = (2 * core + ri) * part
                out[at : at + part, :] = total[2 * xx + core, pl.ds(start_row, part), :]


def unpack_kernel(*refs):
    pieces, out, rows, halves = refs[:8], refs[8], refs[9], refs[10:]
    y, _, x, c = place()
    cells, channels = out.shape
    half = channels // 2
    part = half // 8
    for number, piece in enumerate(pieces):
        yy = y if number // 4 == 0 else 1 - y
        xx = x if number // 2 % 2 == 0 else 1 - x
        cc = c if number % 2 == 0 else 1 - c
        at = pl.multiple_of((4 * yy + 2 * xx + cc) * part, part)
        for ri in range(2):
            start = pl.multiple_of((2 * c + ri) * part, part)
            rows[pl.ds(at + ri * half, part), :] = piece[pl.ds(start, part), :]
    lanes = cells // 8
    for j in range(8):
        for ri in range(2):
            block = rows[ri * half : (ri + 1) * half, j * lanes : (j + 1) * lanes].T
            halves[ri][pl.ds(j, lanes, stride=8), :] = block
    for ri in range(2):
        out[:, ri * half : (ri + 1) * half] = halves[ri][...]


VMEM = pl.BlockSpec(memory_space=pltpu.VMEM)
SMEM = pl.BlockSpec(memory_space=pltpu.SMEM)
BOTH = ("pulse", "grid")


def local(slabs, orbitals, potential, pulse, projectors, couplings, sphere_points, atom_count):
    _, nx, ny, channels = orbitals.shape
    cells = nx * ny
    atoms, k, size = projectors.shape
    part = channels // 16
    y, g = lax.axis_index("pulse"), lax.axis_index("grid")
    quads = slabs // GROUP
    quad = g // GROUP

    def permute(value, target):
        pairs = []
        for p in range(2):
            for s in range(slabs):
                to = target(p, s)
                if to is not None:
                    pairs.append((p * slabs + s, to[0] * slabs + to[1]))
        return lax.ppermute(value, BOTH, pairs)

    def swap_core(value):
        return permute(value, lambda p, s: (p, s ^ 1))

    def shift(value, by):
        return permute(value, lambda p, s: (p, s + by) if 0 <= s + by < slabs else None)

    bundle = jax.ShapeDtypeStruct((5 * channels // 16, cells), F32)
    near, far, heavy = pl.pallas_call(
        pack_kernel,
        out_shape=(bundle, bundle, jax.ShapeDtypeStruct((32, cells), F32)),
        in_specs=[VMEM] * 5 + [SMEM],
        out_specs=[VMEM] * 3,
        scratch_shapes=[pltpu.VMEM((cells, channels // 2), F32), pltpu.VMEM((channels // 2, cells), F32)],
        name="pack",
    )(orbitals.reshape(cells, channels), potential.reshape(nx, ny), projectors, couplings, sphere_points, atom_count)

    beside = permute(far, lambda p, s: (p, s ^ 2))
    below1, above1 = shift(near, GROUP), shift(near, -GROUP)
    below2, above2 = shift(beside, GROUP), shift(beside, -GROUP)
    other_pulse = permute(pulse, lambda p, s: (1 - p, s))
    order = []
    for piece in (below1, below2, near, beside, above1, above2):
        order += [piece, swap_core(piece)]

    edge = max(slabs // 8, 1)
    shared_heavy = not (edge == 2 and quads >= 4)
    if shared_heavy:
        everywhere = lax.all_gather(heavy, "grid")
        blank = jnp.zeros((HALO - 1,) + heavy.shape, F32)
        padded = jnp.concatenate([blank, everywhere, blank])
        heavies = [lax.dynamic_slice_in_dim(padded, quad * GROUP, SLOTS - 2)]
        stores = SLOTS - 2
    else:
        crowded = (0, 1, slabs - 2, slabs - 1)
        across = permute(heavy, lambda p, s: (p, s ^ 2) if s in crowded else None)
        x = (g // 2) % 2
        own = ((quad == 0) & (x == 0)) | ((quad == quads - 1) & (x == 1))
        held = jnp.where(own, heavy, across)

        def outward(p, s):
            if s // GROUP == 0 and s % 2 == 1:
                return p, s + GROUP
            if s // GROUP == quads - 1 and s % 2 == 0:
                return p, s - GROUP
            return None

        moved = permute(held, outward)
        held = jnp.where((quad == 0) | (quad == quads - 1), held, moved)
        heavies = [held, swap_core(held)]
        stores = 2

    wide = 3 * atoms * k
    outs = pl.pallas_call(
        functools.partial(evolve_kernel, slabs, shared_heavy),
        out_shape=[jax.ShapeDtypeStruct((4 * part, cells), F32)] * 4 + [jax.ShapeDtypeStruct((2, 128), F32)],
        in_specs=[SMEM] * 2 + [VMEM] * (12 + len(heavies)),
        out_specs=[VMEM] * 5,
        scratch_shapes=[
            pltpu.VMEM((SLOTS, 2 * part, cells), F32),
            pltpu.VMEM((SLOTS, 4 * part, cells), F32),
            pltpu.VMEM((SLOTS, 4 * part, cells), F32),
            pltpu.VMEM((SLOTS, 4 * part, cells), BF16),
            pltpu.VMEM((SLOTS, 8 * part, cells), BF16),
            pltpu.VMEM((GROUP, 4 * part, cells), F32),
            pltpu.VMEM((SLOTS, 3 * LIGHT * k, cells), BF16),
            pltpu.VMEM((stores, wide, cells), BF16),
            pltpu.VMEM((SLOTS, 1, cells), F32),
            pltpu.VMEM((SLOTS, 1, 128), F32),
            pltpu.VMEM((4 * part, cells), F32),
        ],
        compiler_params=pltpu.CompilerParams(vmem_limit_bytes=50 * 2**20),
        name="evolve",
    )(pulse, other_pulse, *order, *heavies)
    moment = outs[4]
    finals = [
        outs[0],
        permute(outs[1], lambda p, s: (p, s ^ 2)),
        permute(outs[2], lambda p, s: (1 - p, s)),
        permute(outs[3], lambda p, s: (1 - p, s ^ 2)),
    ]
    pieces = []
    for piece in finals:
        pieces += [piece, swap_core(piece)]
    plane = pl.pallas_call(
        unpack_kernel,
        out_shape=jax.ShapeDtypeStruct((cells, channels), F32),
        in_specs=[VMEM] * 8,
        out_specs=VMEM,
        scratch_shapes=[pltpu.VMEM((channels, cells), F32)] + [pltpu.VMEM((cells, channels // 2), F32)] * 2,
        name="unpack",
    )(*pieces)

    shares = moment[:, :1]
    step = 1
    while step < quads:
        if quads & (quads - 1) == 0:
            shares = shares + permute(shares, lambda p, s, step=step: (p, s ^ (step * GROUP)))
            step *= 2
        else:
            shares = lax.psum(shares, BOTH) if step == 1 else shares
            step = quads
    if quads & (quads - 1) == 0:
        for target in (lambda p, s: (p, s ^ 1), lambda p, s: (p, s ^ 2), lambda p, s: (1 - p, s)):
            shares = shares + permute(shares, target)
    total = jnp.where(y == 0, shares[0], shares[1])
    dipole = total / (slabs * cells * (channels // 2))
    return plane.reshape(orbitals.shape), dipole.reshape(1)


def solution(mesh):
    placed = (
        P("grid", None, None, None),
        P("grid", None, None),
        P("pulse"),
        P("grid", None, None),
        P("grid", None),
        P("grid", None),
        P("grid"),
    )
    return jax.shard_map(
        functools.partial(local, mesh.shape["grid"]),
        mesh=mesh,
        in_specs=placed,
        out_specs=(P(("pulse", "grid"), None, None, None), P("pulse")),
        check_vma=False,
    )
```

```python
import functools

import jax
import jax.numpy as jnp
from jax import lax
from jax.experimental import pallas as pl
from jax.experimental.pallas import tpu as pltpu
from jax.sharding import PartitionSpec as P


TERMS = 4
TIME_STEP = 0.1
GROUP = 4
HALO = TERMS
SLOTS = GROUP + 2 * HALO
LIGHT = 4
F32 = jnp.float32
BF16 = jnp.bfloat16
NT = (((1,), (1,)), ((), ()))
NN = (((1,), (0,)), ((), ()))


def iota(shape, dim):
    return lax.broadcasted_iota(jnp.int32, shape, dim)


def split(value):
    high = value.astype(BF16)
    return high, (value - high.astype(F32)).astype(BF16)


def place():
    y, g = lax.axis_index("pulse"), lax.axis_index("grid")
    return y, g // GROUP, (g // 2) % 2, g % 2


def pack_kernel(orb, pot, proj, coup, points, count, near, far, packed, rows):
    y, _, x, _ = place()
    cells, channels = orb.shape
    lanes = cells // 8
    half = channels // 2
    first = iota((lanes, half), 1) < half // 2
    for j in range(8):
        chunk = slice(j * lanes, (j + 1) * lanes)
        re, im = orb[chunk, :half], orb[chunk, half:]
        low = jnp.where(first, re, pltpu.roll(im, half // 2, 1))
        high = jnp.where(first, pltpu.roll(re, half // 2, 1), im)
        packed[chunk, :] = jnp.where(y == 0, low, high)
    for j in range(8):
        rows[:, j * lanes : (j + 1) * lanes] = packed[pl.ds(j, lanes, stride=8), :].T
    part = half // 8
    for out, xx in ((near, x), (far, 1 - x)):
        for c in range(2):
            start = pl.multiple_of((2 * xx + c) * part, part)
            out[c * 2 * part : c * 2 * part + part, :] = rows[pl.ds(start, part), :]
            out[c * 2 * part + part : (c + 1) * 2 * part, :] = rows[pl.ds(start + half // 2, part), :]
    nx, ny = pot.shape
    yh = ny // 8
    col = iota((ny, cells), 1)
    pick = (iota((ny, cells), 0) == (col % lanes) % yh * 8 + col // lanes).astype(F32)
    spread = lax.dot_general(pot[...], pick, NN, precision=lax.Precision.HIGHEST, preferred_element_type=F32)
    keep = iota((nx, cells), 0) == (iota((nx, cells), 1) % lanes) // yh
    pot_row = jnp.sum(jnp.where(keep, spread, 0.0), axis=0, keepdims=True)
    k, atoms = coup.shape
    pick = (iota((atoms, atoms * k), 0) == iota((atoms, atoms * k), 1) // k).astype(F32)
    spread = lax.dot_general(coup[...], pick, NN, precision=lax.Precision.HIGHEST, preferred_element_type=F32)
    column = iota((k, atoms * k), 1)
    keep = (iota((k, atoms * k), 0) == column % k) & (column // k < count[0])
    weight_row = jnp.sum(jnp.where(keep, spread, 0.0), axis=0, keepdims=True)
    size = points.shape[1]
    base = 4 * part
    for out in (near, far):
        for a in range(LIGHT):
            out[base : base + k, a * size : (a + 1) * size] = proj[a].astype(F32)
            out[base + k : base + k + 1, a * size : (a + 1) * size] = points[a : a + 1, :].astype(F32)
        out[base + k + 1 : base + k + 2, :] = pot_row
        out[base + k + 2 : base + k + 3, :] = jnp.zeros((1, cells), F32)
        out[base + k + 2 : base + k + 3, : atoms * k] = weight_row
        out[base + k + 3 : base + k + 8, :] = jnp.zeros((5, cells), F32)


def rest_kernel(proj, points, near, rest):
    atoms, k, size = proj.shape
    groups = atoms // LIGHT - 1
    for group in range(groups):
        for a in range(LIGHT):
            source = (group + 1) * LIGHT + a
            rest[group * k : (group + 1) * k, a * size : (a + 1) * size] = proj[source].astype(F32)
            rest[groups * k + group : groups * k + group + 1, a * size : (a + 1) * size] = (
                points[source : source + 1, :].astype(F32)
            )
    used = groups * (k + 1)
    rest[used:, :] = near[near.shape[0] - rest.shape[0] + used :, :]


def matrix_of(proj, points, size):
    k = proj.shape[0]
    parts = []
    for a in range(LIGHT):
        values = proj[:, a * size : (a + 1) * size]
        cell = points[:, a * size : (a + 1) * size].astype(jnp.int32)
        low, lane = cell & 7, cell >> 3
        tall = jnp.concatenate([jnp.where(low == j, values, 0.0) for j in range(8)], axis=0).astype(BF16)
        hot = jnp.where(iota((128, size), 0) == lane, 1.0, 0.0).astype(BF16)
        sums = lax.dot_general(tall, hot, NT, preferred_element_type=F32)
        parts.append(jnp.concatenate([sums[j * k : (j + 1) * k, :] for j in range(8)], axis=1))
    return jnp.concatenate(parts, axis=0)


def matrices_kernel(*refs):
    bundles, out = refs[:-1], refs[-1]
    for number, bundle in enumerate(bundles):
        base = bundle.shape[0] - 16
        k, size = 8, bundle.shape[1] // LIGHT
        high, low = split(matrix_of(bundle[base : base + k, :], bundle[base + k : base + k + 1, :], size))
        span = LIGHT * k
        out[number, :span] = high
        out[number, span : 2 * span] = low
        out[number, 2 * span :] = high


def roll_lanes(value, shift):
    return pltpu.roll(value, shift % value.shape[1], 1)


def evolve_kernel(slabs, shared_heavy, *refs):
    own_pulse, other_pulse = refs[:2]
    bundles, ready = refs[2:14], refs[14:16]
    heavies = refs[16:17] if shared_heavy else refs[16:18]
    refs = refs[16 + len(heavies) :]
    outs, moment = refs[:4], refs[4]
    start, term1, term2, term3, start_split, split1, split2, total, light, full, pots, weights = refs[5:]
    y, quad, x, c = place()
    quads = slabs // GROUP
    part = start.shape[1] // 2
    cells = start.shape[2]
    k = 8
    size = cells // LIGHT
    base = 4 * part
    span = LIGHT * k
    edge = max(slabs // 8, 1)
    has_low, has_high = quad > 0, quad < quads - 1

    for number, bundle in enumerate(bundles):
        direction, xf, cf = number // 4, number // 2 % 2, number % 2
        slot = direction * GROUP + 2 * (x if xf == 0 else 1 - x) + (c if cf == 0 else 1 - c)
        rows = bundle[pl.ds(pl.multiple_of(c * 2 * part, 2 * part), 2 * part), :]
        start[slot] = rows
        high, low = split(rows)
        start_split[slot, : 2 * part] = high
        start_split[slot, 2 * part :] = low
        pots[slot] = bundle[base + k + 1 : base + k + 2, :]
        weights[slot] = bundle[base + k + 2 : base + k + 3, : 4 * span]

        if direction == 1:
            light[slot] = ready[0][2 * xf + cf]
        elif xf == 0:
            light[slot] = ready[1][direction + cf]
        else:

            @pl.when((has_low if direction == 0 else has_high) & (slot > 0) & (slot < SLOTS - 1))
            def _(bundle=bundle, slot=slot):
                high, low = split(matrix_of(bundle[base : base + k, :], bundle[base + k : base + k + 1, :], size))
                light[slot, :span] = high
                light[slot, span : 2 * span] = low
                light[slot, 2 * span :] = high

    def plane_of(slot):
        return quad * GROUP + slot - HALO

    def is_heavy(slot):
        plane = plane_of(slot)
        return (plane < edge) | (plane >= slabs - edge)

    extra = 3 * span

    def build_full(store, source):
        for group in range(3):
            high, low = split(matrix_of(source(group * k, k), source(3 * k + group, 1), size))
            for part_of, value in enumerate((high, low, high)):
                at = part_of * extra + group * span
                full[store, at : at + span] = value

    if shared_heavy:

        def store_of(slot):
            return slot - 1

        for slot in range(1, SLOTS - 1):
            exists = (plane_of(slot) >= 0) & (plane_of(slot) < slabs)

            @pl.when(exists & is_heavy(slot))
            def _(slot=slot):
                build_full(slot - 1, lambda at, n: heavies[0][slot - 1, at : at + n, :])
    else:
        ends = (quad == 0) | (quad == quads - 1)
        beside = (quad == 1) | (quad == quads - 2)
        low_end = quad <= 1
        first_slot = jnp.where(low_end, HALO, HALO + 2)

        def store_of(slot):
            return jnp.where(ends, slot - first_slot, 0)

        @pl.when(ends)
        def _():
            for cf in range(2):
                build_full(c if cf == 0 else 1 - c, lambda at, n, cf=cf: heavies[cf][at : at + n, :])

        @pl.when(beside)
        def _():
            mine = (c == 1) == low_end
            build_full(0, lambda at, n: jnp.where(mine, heavies[0][at : at + n, :], heavies[1][at : at + n, :]))

    for missing, slot in ((jnp.logical_not(has_low), HALO - 1), (jnp.logical_not(has_high), HALO + GROUP)):

        @pl.when(missing)
        def _(slot=slot):
            for term in (term1, term2, term3):
                term[slot] = jnp.zeros(term.shape[1:], F32)

    def coefficients(halves, matrix, weight, count, width, factor):
        r = lax.dot_general(halves, matrix, NT, preferred_element_type=F32)
        coeffs = r[:count, :width] + r[count:, :width] + r[:count, width:]
        sign = jnp.where(iota((count, width), 0) < count // 2, -factor, factor)
        high, low = split(coeffs * weight * sign)
        return jnp.concatenate([high, high, low], axis=1)

    lane = iota((1, 128), 1)
    groups_y = 4
    wrap_up, wrap_down = lane % groups_y == groups_y - 1, lane % groups_y == 0

    def columns(j):
        return slice(j * 128, (j + 1) * 128)

    def neighbours(field, slot, j, v):
        around = field[slot - 1, :, columns(j)] + field[slot + 1, :, columns(j)]
        around += roll_lanes(v, groups_y) + roll_lanes(v, -groups_y)
        w = field[slot, :, columns((j + 1) % 8)]
        around += w if j < 7 else jnp.where(wrap_up, roll_lanes(w, groups_y - 1), roll_lanes(w, -1))
        w = field[slot, :, columns((j - 1) % 8)]
        return around + (w if j > 0 else jnp.where(wrap_down, roll_lanes(w, 1 - groups_y), roll_lanes(w, 1)))

    def pulse_field(slot, p):
        strength = jnp.where(y == p, own_pulse[0], other_pulse[0])
        position = (plane_of(slot).astype(F32) + 0.5) / slabs
        return strength * 4.0 * (position - 0.5)

    def put(term, halves, slot, rows, cols, value):
        term[slot, rows, cols] = value
        high, low = split(value)
        halves[slot, rows, cols] = high
        halves[slot, slice(4 * part + rows.start, 4 * part + rows.stop), cols] = low

    def bounds(order):
        reach = TERMS - order
        low = jnp.where(has_low, HALO - reach, HALO)
        high = jnp.where(has_high, HALO + GROUP + reach, HALO + GROUP)
        return low, high

    def sweep(order, halves, count, apply, correct):
        factor = TIME_STEP / order
        low, high = bounds(order)

        def ahead(slot):
            return coefficients(
                halves[slot], light[slot, : 2 * span, :], weights[slot][:, :span], count, span, factor
            )

        def body(slot, wide):
            following = ahead(jnp.minimum(slot + 1, high - 1))
            apply(slot, lax.dot_general(wide, light[slot], NN, preferred_element_type=F32))

            @pl.when(is_heavy(slot))
            def _():
                store = store_of(slot)
                wide = coefficients(
                    halves[slot], full[store, : 2 * extra, :], weights[slot][:, span:], count, extra, factor
                )
                correct(slot, lax.dot_general(wide, full[store], NN, preferred_element_type=F32))

            return following

        lax.fori_loop(low, high, body, ahead(low))

    re, im = slice(0, 2 * part), slice(2 * part, 4 * part)

    def apply_first(slot, projected):
        fields = [pulse_field(slot, p) for p in range(2)]
        pot = pots[slot] + 3.0
        for j in range(8):
            cols = columns(j)
            v = start[slot, :, cols]
            around = neighbours(start, slot, j, v)
            sign = jnp.where(iota(v.shape, 0) < part, -TIME_STEP, TIME_STEP)
            image = sign * (pot[:, cols] * v - 0.5 * around) + projected[:, cols]
            turned = sign * v
            for p in range(2):
                value = image + fields[p] * turned
                put(term1, split1, slot, slice(p * part, (p + 1) * part), cols, value[part:])
                put(term1, split1, slot, slice((2 + p) * part, (3 + p) * part), cols, value[:part])

    def correct_first(slot, projected):
        for j in range(8):
            cols = columns(j)
            for p in range(2):
                for ri in range(2):
                    rows = slice((2 * ri + p) * part, (2 * ri + p + 1) * part)
                    more = projected[(1 - ri) * part : (2 - ri) * part, cols]
                    put(term1, split1, slot, rows, cols, term1[slot, rows, cols] + more)

    sweep(1, start_split, 2 * part, apply_first, correct_first)

    def image_of(order, source, slot, projected):
        factor = TIME_STEP / order
        fields = [pulse_field(slot, p) for p in range(2)]
        row = iota((4 * part, 128), 0)
        sign = jnp.where(row < 2 * part, -factor, factor)
        shift = sign * jnp.where(row // part % 2 == 0, 3.0 + fields[0], 3.0 + fields[1])
        half = -0.5 * sign
        for j in range(8):
            cols = columns(j)
            v = source[slot, :, cols]
            around = neighbours(source, slot, j, v)
            yield cols, (pots[slot][:, cols] * sign + shift) * v + half * around + projected[:, cols]

    def later(order, source, halves, target, target_split):
        def apply(slot, projected):
            for cols, image in image_of(order, source, slot, projected):
                put(target, target_split, slot, re, cols, image[im])
                put(target, target_split, slot, im, cols, image[re])

        def correct(slot, projected):
            for j in range(8):
                cols = columns(j)
                put(target, target_split, slot, re, cols, target[slot, re, cols] + projected[im, cols])
                put(target, target_split, slot, im, cols, target[slot, im, cols] + projected[re, cols])

        sweep(order, halves, 4 * part, apply, correct)

    later(2, term1, split1, term2, split2)
    later(3, term2, split2, term3, split1)

    def apply_last(slot, projected):
        at = slot - HALO
        for cols, image in image_of(TERMS, term3, slot, projected):
            terms = term1[slot, :, cols] + term2[slot, :, cols] + term3[slot, :, cols]
            for ri in range(2):
                begun = start[slot, ri * part : (ri + 1) * part, cols]
                for p in range(2):
                    rows = slice((2 * ri + p) * part, (2 * ri + p + 1) * part)
                    turned = slice((2 - 2 * ri + p) * part, (3 - 2 * ri + p) * part)
                    total[at, rows, cols] = begun + terms[rows] + image[turned]

    def correct_last(slot, projected):
        at = slot - HALO
        total[at, re] += projected[im]
        total[at, im] += projected[re]

    sweep(TERMS, split1, 4 * part, apply_last, correct_last)

    shares = jnp.zeros((4 * part, 128), F32)
    for slot in range(GROUP):
        position = (plane_of(slot + HALO).astype(F32) + 0.5) / slabs
        squares = jnp.zeros((4 * part, 128), F32)
        for j in range(8):
            v = total[slot, :, columns(j)]
            squares += v * v
        shares += position * squares
    for p in range(2):
        rows = slice(p * part, (p + 1) * part)
        value = jnp.sum(shares[rows] + shares[slice((2 + p) * part, (3 + p) * part)])
        moment[p : p + 1, :] = jnp.full((1, 128), value, F32)
    for number, out in enumerate(outs):
        yy = y if number // 2 == 0 else 1 - y
        xx = x if number % 2 == 0 else 1 - x
        for core in range(2):
            for ri in range(2):
                start_row = pl.multiple_of((2 * ri + yy) * part, part)
                at = (2 * core + ri) * part
                out[at : at + part, :] = total[2 * xx + core, pl.ds(start_row, part), :]


def unpack_kernel(*refs):
    pieces, out, rows, halves = refs[:8], refs[8], refs[9], refs[10:]
    y, _, x, c = place()
    cells, channels = out.shape
    half = channels // 2
    part = half // 8
    for number, piece in enumerate(pieces):
        yy = y if number // 4 == 0 else 1 - y
        xx = x if number // 2 % 2 == 0 else 1 - x
        cc = c if number % 2 == 0 else 1 - c
        at = pl.multiple_of((4 * yy + 2 * xx + cc) * part, part)
        for ri in range(2):
            start = pl.multiple_of((2 * c + ri) * part, part)
            rows[pl.ds(at + ri * half, part), :] = piece[pl.ds(start, part), :]
    lanes = cells // 8
    for j in range(8):
        for ri in range(2):
            block = rows[ri * half : (ri + 1) * half, j * lanes : (j + 1) * lanes].T
            halves[ri][pl.ds(j, lanes, stride=8), :] = block
    for ri in range(2):
        out[:, ri * half : (ri + 1) * half] = halves[ri][...]


VMEM = pl.BlockSpec(memory_space=pltpu.VMEM)
SMEM = pl.BlockSpec(memory_space=pltpu.SMEM)
BOTH = ("pulse", "grid")


def local(slabs, orbitals, potential, pulse, projectors, couplings, sphere_points, atom_count):
    _, nx, ny, channels = orbitals.shape
    cells = nx * ny
    atoms, k, size = projectors.shape
    part = channels // 16
    y, g = lax.axis_index("pulse"), lax.axis_index("grid")
    quads = slabs // GROUP
    quad = g // GROUP

    def permute(value, target):
        pairs = []
        for p in range(2):
            for s in range(slabs):
                to = target(p, s)
                if to is not None:
                    pairs.append((p * slabs + s, to[0] * slabs + to[1]))
        return lax.ppermute(value, BOTH, pairs)

    def swap_core(value):
        return permute(value, lambda p, s: (p, s ^ 1))

    def shift(value, by):
        return permute(value, lambda p, s: (p, s + by) if 0 <= s + by < slabs else None)

    bundle = jax.ShapeDtypeStruct((5 * channels // 16, cells), F32)
    near, far = pl.pallas_call(
        pack_kernel,
        out_shape=(bundle, bundle),
        in_specs=[VMEM] * 5 + [SMEM],
        out_specs=[VMEM] * 2,
        scratch_shapes=[pltpu.VMEM((cells, channels // 2), F32), pltpu.VMEM((channels // 2, cells), F32)],
        name="pack",
    )(orbitals.reshape(cells, channels), potential.reshape(nx, ny), projectors, couplings.T, sphere_points, atom_count)
    beside = permute(far, lambda p, s: (p, s ^ 2))
    below1, above1 = shift(near, GROUP), shift(near, -GROUP)
    heavy = pl.pallas_call(
        rest_kernel,
        out_shape=jax.ShapeDtypeStruct((32, cells), F32),
        in_specs=[VMEM] * 3,
        out_specs=VMEM,
        name="rest",
    )(projectors, sphere_points, near)
    pulse_sent, heavy = lax.optimization_barrier((pulse, heavy))
    below2, above2 = shift(beside, GROUP), shift(beside, -GROUP)
    other_pulse = permute(pulse_sent, lambda p, s: (1 - p, s))
    order = []
    for piece in (below1, below2, near, beside, above1, above2):
        order += [piece, swap_core(piece)]

    def matrices(bundles):
        return pl.pallas_call(
            matrices_kernel,
            out_shape=jax.ShapeDtypeStruct((len(bundles), 3 * LIGHT * k, cells), BF16),
            in_specs=[VMEM] * len(bundles),
            out_specs=VMEM,
            name="matrices",
        )(*bundles)

    ready = [matrices(order[4:8]), matrices(order[:2] + order[8:10])]

    edge = max(slabs // 8, 1)
    shared_heavy = not (edge == 2 and quads >= 4)
    if shared_heavy:
        everywhere = lax.all_gather(heavy, "grid")
        blank = jnp.zeros((HALO - 1,) + heavy.shape, F32)
        padded = jnp.concatenate([blank, everywhere, blank])
        heavies = [lax.dynamic_slice_in_dim(padded, quad * GROUP, SLOTS - 2)]
        stores = SLOTS - 2
    else:
        crowded = (0, 1, slabs - 2, slabs - 1)
        across = permute(heavy, lambda p, s: (p, s ^ 2) if s in crowded else None)
        x = (g // 2) % 2
        own = ((quad == 0) & (x == 0)) | ((quad == quads - 1) & (x == 1))
        held = jnp.where(own, heavy, across)

        def outward(p, s):
            if s // GROUP == 0 and s % 2 == 1:
                return p, s + GROUP
            if s // GROUP == quads - 1 and s % 2 == 0:
                return p, s - GROUP
            return None

        moved = permute(held, outward)
        held = jnp.where((quad == 0) | (quad == quads - 1), held, moved)
        heavies = [held, swap_core(held)]
        stores = 2

    wide = 3 * (atoms - LIGHT) * k
    outs = pl.pallas_call(
        functools.partial(evolve_kernel, slabs, shared_heavy),
        out_shape=[jax.ShapeDtypeStruct((4 * part, cells), F32)] * 4 + [jax.ShapeDtypeStruct((2, 128), F32)],
        in_specs=[SMEM] * 2 + [VMEM] * (14 + len(heavies)),
        out_specs=[VMEM] * 5,
        scratch_shapes=[pltpu.VMEM((SLOTS, 2 * part, cells), F32)]
        + [pltpu.VMEM((SLOTS, 4 * part, cells), F32)] * 3
        + [pltpu.VMEM((SLOTS, 4 * part, cells), BF16)]
        + [pltpu.VMEM((SLOTS, 8 * part, cells), BF16)] * 2
        + [
            pltpu.VMEM((GROUP, 4 * part, cells), F32),
            pltpu.VMEM((SLOTS, 3 * LIGHT * k, cells), BF16),
            pltpu.VMEM((stores, wide, cells), BF16),
            pltpu.VMEM((SLOTS, 1, cells), F32),
            pltpu.VMEM((SLOTS, 1, 128), F32),
        ],
        compiler_params=pltpu.CompilerParams(vmem_limit_bytes=(36 if not shared_heavy else 50) * 2**20),
        name="evolve",
    )(pulse, other_pulse, *order, *ready, *heavies)
    moment = outs[4]
    finals = [
        outs[0],
        permute(outs[1], lambda p, s: (p, s ^ 2)),
        permute(outs[2], lambda p, s: (1 - p, s)),
        permute(outs[3], lambda p, s: (1 - p, s ^ 2)),
    ]
    devices = 2 * slabs
    shares = jnp.broadcast_to(jnp.concatenate([moment[0], moment[1]])[None, None, :], (devices, 1, 256))
    shares = lax.all_to_all(shares, BOTH, 0, 0)
    *finals, shares = lax.optimization_barrier((*finals, shares))
    pieces = []
    for piece in finals:
        pieces += [piece, swap_core(piece)]
    plane = pl.pallas_call(
        unpack_kernel,
        out_shape=jax.ShapeDtypeStruct((cells, channels), F32),
        in_specs=[VMEM] * 8,
        out_specs=VMEM,
        scratch_shapes=[pltpu.VMEM((channels, cells), F32)] + [pltpu.VMEM((cells, channels // 2), F32)] * 2,
        compiler_params=pltpu.CompilerParams(vmem_limit_bytes=16 * 2**20),
        name="unpack",
    )(*pieces)

    total = jnp.where(y == 0, jnp.sum(shares[:, 0, 0]), jnp.sum(shares[:, 0, 128]))
    dipole = total / (slabs * cells * (channels // 2))
    return plane.reshape(orbitals.shape), dipole.reshape(1)


def solution(mesh):
    placed = (
        P("grid", None, None, None),
        P("grid", None, None),
        P("pulse"),
        P("grid", None, None),
        P("grid", None),
        P("grid", None),
        P("grid"),
    )
    return jax.shard_map(
        functools.partial(local, mesh.shape["grid"]),
        mesh=mesh,
        in_specs=placed,
        out_specs=(P(("pulse", "grid"), None, None, None), P("pulse")),
        check_vma=False,
    )
```

```python
import functools

import jax
import jax.numpy as jnp
from jax import lax
from jax.experimental import pallas as pl
from jax.experimental.pallas import tpu as pltpu
from jax.sharding import PartitionSpec as P


TERMS = 4
TIME_STEP = 0.1
GROUP = 4
HALO = TERMS
SLOTS = GROUP + 2 * HALO
LIGHT = 4
F32 = jnp.float32
BF16 = jnp.bfloat16
NT = (((1,), (1,)), ((), ()))
NN = (((1,), (0,)), ((), ()))


def iota(shape, dim):
    return lax.broadcasted_iota(jnp.int32, shape, dim)


def split(value):
    high = value.astype(BF16)
    return high, (value - high.astype(F32)).astype(BF16)


def place():
    y, g = lax.axis_index("pulse"), lax.axis_index("grid")
    return y, g // GROUP, (g // 2) % 2, g % 2


def pack_kernel(orb, pot, proj, coup, points, count, near, far, packed, rows):
    y, _, x, _ = place()
    cells, channels = orb.shape
    lanes = cells // 8
    half = channels // 2
    first = iota((lanes, half), 1) < half // 2
    for j in range(8):
        chunk = slice(j * lanes, (j + 1) * lanes)
        re, im = orb[chunk, :half], orb[chunk, half:]
        low = jnp.where(first, re, pltpu.roll(im, half // 2, 1))
        high = jnp.where(first, pltpu.roll(re, half // 2, 1), im)
        packed[chunk, :] = jnp.where(y == 0, low, high)
    for j in range(8):
        rows[:, j * lanes : (j + 1) * lanes] = packed[pl.ds(j, lanes, stride=8), :].T
    part = half // 8
    for out, xx in ((near, x), (far, 1 - x)):
        for c in range(2):
            start = pl.multiple_of((2 * xx + c) * part, part)
            out[c * 2 * part : c * 2 * part + part, :] = rows[pl.ds(start, part), :]
            out[c * 2 * part + part : (c + 1) * 2 * part, :] = rows[pl.ds(start + half // 2, part), :]
    nx, ny = pot.shape
    yh = ny // 8
    col = iota((ny, cells), 1)
    pick = (iota((ny, cells), 0) == (col % lanes) % yh * 8 + col // lanes).astype(F32)
    spread = lax.dot_general(pot[...], pick, NN, precision=lax.Precision.HIGHEST, preferred_element_type=F32)
    keep = iota((nx, cells), 0) == (iota((nx, cells), 1) % lanes) // yh
    pot_row = jnp.sum(jnp.where(keep, spread, 0.0), axis=0, keepdims=True)
    k, atoms = coup.shape
    pick = (iota((atoms, atoms * k), 0) == iota((atoms, atoms * k), 1) // k).astype(F32)
    spread = lax.dot_general(coup[...], pick, NN, precision=lax.Precision.HIGHEST, preferred_element_type=F32)
    column = iota((k, atoms * k), 1)
    keep = (iota((k, atoms * k), 0) == column % k) & (column // k < count[0])
    weight_row = jnp.sum(jnp.where(keep, spread, 0.0), axis=0, keepdims=True)
    size = points.shape[1]
    base = 4 * part
    for out in (near, far):
        for a in range(LIGHT):
            out[base : base + k, a * size : (a + 1) * size] = proj[a].astype(F32)
            out[base + k : base + k + 1, a * size : (a + 1) * size] = points[a : a + 1, :].astype(F32)
        out[base + k + 1 : base + k + 2, :] = pot_row
        out[base + k + 2 : base + k + 3, :] = jnp.zeros((1, cells), F32)
        out[base + k + 2 : base + k + 3, : atoms * k] = weight_row
        out[base + k + 3 : base + k + 8, :] = jnp.zeros((5, cells), F32)


def rest_kernel(proj, points, near, rest):
    atoms, k, size = proj.shape
    groups = atoms // LIGHT - 1
    for group in range(groups):
        for a in range(LIGHT):
            source = (group + 1) * LIGHT + a
            rest[group * k : (group + 1) * k, a * size : (a + 1) * size] = proj[source].astype(F32)
            rest[groups * k + group : groups * k + group + 1, a * size : (a + 1) * size] = (
                points[source : source + 1, :].astype(F32)
            )
    used = groups * (k + 1)
    spare = rest.shape[0] - used
    rest[used:, :] = near[near.shape[0] - spare :, :]


def matrix_of(proj, points, size):
    k = proj.shape[0]
    parts = []
    for a in range(LIGHT):
        values = proj[:, a * size : (a + 1) * size]
        cell = points[:, a * size : (a + 1) * size].astype(jnp.int32)
        low, lane = cell & 7, cell >> 3
        tall = jnp.concatenate([jnp.where(low == j, values, 0.0) for j in range(8)], axis=0).astype(BF16)
        hot = jnp.where(iota((128, size), 0) == lane, 1.0, 0.0).astype(BF16)
        sums = lax.dot_general(tall, hot, NT, preferred_element_type=F32)
        parts.append(jnp.concatenate([sums[j * k : (j + 1) * k, :] for j in range(8)], axis=1))
    return jnp.concatenate(parts, axis=0)


def roll_lanes(value, shift):
    return pltpu.roll(value, shift % value.shape[1], 1)


def evolve_kernel(slabs, shared_heavy, *refs):
    own_pulse, other_pulse = refs[:2]
    bundles = refs[2:14]
    heavies = refs[14:15] if shared_heavy else refs[14:16]
    refs = refs[14 + len(heavies) :]
    outs, moment = refs[:4], refs[4]
    start, term1, term2, term3, start_split, split1, split2, total, light, full, pots, weights, coming = refs[5:]
    y, quad, x, c = place()
    quads = slabs // GROUP
    part = start.shape[1] // 2
    cells = start.shape[2]
    k = 8
    size = cells // LIGHT
    base = 4 * part
    span = LIGHT * k
    edge = max(slabs // 8, 1)
    has_low, has_high = quad > 0, quad < quads - 1

    for number, bundle in enumerate(bundles):
        direction, xf, cf = number // 4, number // 2 % 2, number % 2
        slot = direction * GROUP + 2 * (x if xf == 0 else 1 - x) + (c if cf == 0 else 1 - c)
        rows = bundle[pl.ds(pl.multiple_of(c * 2 * part, 2 * part), 2 * part), :]
        start[slot] = rows
        high, low = split(rows)
        start_split[slot, : 2 * part] = high
        start_split[slot, 2 * part :] = low
        pots[slot] = bundle[base + k + 1 : base + k + 2, :]
        weights[slot] = bundle[base + k + 2 : base + k + 3, : 4 * span]

        def build(bundle=bundle, slot=slot):
            high, low = split(matrix_of(bundle[base : base + k, :], bundle[base + k : base + k + 1, :], size))
            light[slot, :span] = high
            light[slot, span : 2 * span] = low
            light[slot, 2 * span :] = high

        if direction == 1:
            build()
        else:
            pl.when((has_low if direction == 0 else has_high) & (slot > 0) & (slot < SLOTS - 1))(build)

    def plane_of(slot):
        return quad * GROUP + slot - HALO

    def is_heavy(slot):
        plane = plane_of(slot)
        return (plane < edge) | (plane >= slabs - edge)

    wide = 4 * span

    def build_full(store, source, slot):
        for part_of in range(3):
            full[store, part_of * wide : part_of * wide + span] = light[slot, part_of * span : (part_of + 1) * span]
        for group in range(3):
            high, low = split(matrix_of(source(group * k, k), source(3 * k + group, 1), size))
            for part_of, value in enumerate((high, low, high)):
                at = part_of * wide + (group + 1) * span
                full[store, at : at + span] = value

    if shared_heavy:

        def store_of(slot):
            return slot - 1

        for slot in range(1, SLOTS - 1):
            exists = (plane_of(slot) >= 0) & (plane_of(slot) < slabs)

            @pl.when(exists & is_heavy(slot))
            def _(slot=slot):
                build_full(slot - 1, lambda at, n: heavies[0][slot - 1, at : at + n, :], slot)
    else:
        ends = (quad == 0) | (quad == quads - 1)
        beside = (quad == 1) | (quad == quads - 2)
        low_end = quad <= 1
        first_slot = jnp.where(low_end, HALO, HALO + 2)

        def store_of(slot):
            return jnp.where(ends, slot - first_slot, 0)

        @pl.when(ends)
        def _():
            for cf in range(2):
                core = c if cf == 0 else 1 - c
                build_full(core, lambda at, n, cf=cf: heavies[cf][at : at + n, :], first_slot + core)

        @pl.when(beside)
        def _():
            mine = (c == 1) == low_end
            lone = jnp.where(low_end, 1, SLOTS - 2)
            build_full(0, lambda at, n: jnp.where(mine, heavies[0][at : at + n, :], heavies[1][at : at + n, :]), lone)

    for missing, slot in ((jnp.logical_not(has_low), HALO - 1), (jnp.logical_not(has_high), HALO + GROUP)):

        @pl.when(missing)
        def _(slot=slot):
            for term in (term1, term2, term3):
                term[slot] = jnp.zeros(term.shape[1:], F32)

    def coefficients(halves, matrix, weight, count, width, factor):
        r = lax.dot_general(halves, matrix, NT, preferred_element_type=F32)
        coeffs = r[:count, :width] + r[count:, :width] + r[:count, width:]
        sign = jnp.where(iota((count, width), 0) < count // 2, -factor, factor)
        high, low = split(coeffs * weight * sign)
        return jnp.concatenate([high, high, low], axis=1)

    lane = iota((1, 128), 1)
    groups_y = 4
    wrap_up, wrap_down = lane % groups_y == groups_y - 1, lane % groups_y == 0

    def columns(j):
        return slice(j * 128, (j + 1) * 128)

    def block_of(field, slot, rows):
        values = [field[slot, rows, columns(j)] for j in range(8)]
        beyond = [field[slot - 1, rows, columns(j)] + field[slot + 1, rows, columns(j)] for j in range(8)]
        for j, v in enumerate(values):
            around = beyond[j] + (roll_lanes(v, groups_y) + roll_lanes(v, -groups_y))
            w = values[(j + 1) % 8]
            around += w if j < 7 else jnp.where(wrap_up, roll_lanes(w, groups_y - 1), roll_lanes(w, -1))
            w = values[(j - 1) % 8]
            around += w if j > 0 else jnp.where(wrap_down, roll_lanes(w, 1 - groups_y), roll_lanes(w, 1))
            yield columns(j), v, around

    def pulse_field(slot, p):
        strength = jnp.where(y == p, own_pulse[0], other_pulse[0])
        position = (plane_of(slot).astype(F32) + 0.5) / slabs
        return strength * 4.0 * (position - 0.5)

    def put(term, halves, slot, pieces):
        halved = [split(value) for _, _, value in pieces]
        for (rows, cols, value), (high, low) in zip(pieces, halved):
            term[slot, rows, cols] = value
            halves[slot, rows, cols] = high
            halves[slot, slice(4 * part + rows.start, 4 * part + rows.stop), cols] = low

    def bounds(order):
        reach = TERMS - order
        low = jnp.where(has_low, HALO - reach, HALO)
        high = jnp.where(has_high, HALO + GROUP + reach, HALO + GROUP)
        return low, high

    def sweep(order, halves, count, apply, correct):
        factor = TIME_STEP / order
        low, high = bounds(order)

        begin = jnp.where(has_high, low, low - low % 2)
        number = (high - begin + 1) // 2

        def pair(i):
            return jnp.clip(begin + 2 * i, low, high - 1), jnp.minimum(begin + 2 * i + 1, high - 1)

        def ahead(i):
            for side, slot in enumerate(pair(i)):
                coming[i % 2, side, :count] = coefficients(
                    halves[slot], light[slot, : 2 * span, :], weights[slot][:, :span], count, span, factor
                )

        def whole(slot, beyond):
            store = store_of(slot)
            weight = jnp.where(iota((1, wide), 1) < span, 0.0, weights[slot]) if beyond else weights[slot]
            right = coefficients(halves[slot], full[store, : 2 * wide, :], weight, count, wide, factor)
            return lax.dot_general(right, full[store], NN, preferred_element_type=F32)

        def body(i, carry):
            slots = pair(i)
            distinct = slots[0] != slots[1]
            both = is_heavy(slots[0]) & is_heavy(slots[1]) & distinct

            @pl.when(jnp.logical_not(both))
            def _():
                ahead(i + 1)
                for side, slot in enumerate(slots):
                    apply(
                        slot,
                        lax.dot_general(coming[i % 2, side, :count], light[slot], NN, preferred_element_type=F32),
                    )

            @pl.when(both)
            def _():
                ahead(i + 1)
                for slot in slots:
                    apply(slot, whole(slot, False))

            for side, slot in enumerate(slots):

                @pl.when(is_heavy(slot) & jnp.logical_not(both) & (distinct | (side == 0)))
                def _(slot=slot):
                    correct(slot, whole(slot, True))

            return carry

        ahead(0)
        lax.fori_loop(0, number, body, 0)

    def blocks():
        for ri in range(2):
            for p in range(2):
                here, there = (2 * ri + p) * part, (2 * (1 - ri) + p) * part
                yield ri, p, slice(here, here + part), slice(there, there + part)

    def apply_first(slot, projected):
        for ri in range(2):
            sign = TIME_STEP if ri else -TIME_STEP
            rows = slice(ri * part, (ri + 1) * part)
            pot = (pots[slot] + 3.0) * sign
            images = [
                (cols, pot[:, cols] * v - (0.5 * sign) * around + projected[rows, cols], v)
                for cols, v, around in block_of(start, slot, rows)
            ]
            for p in range(2):
                there = (2 * (1 - ri) + p) * part
                field = pulse_field(slot, p) * sign
                there = slice(there, there + part)
                put(term1, split1, slot, [(there, cols, image + field * v) for cols, image, v in images])

    def correct_with(term, halves, slot, rows, there, projected):
        put(
            term, halves, slot,
            [(there, columns(j), term[slot, there, columns(j)] + projected[rows, columns(j)]) for j in range(8)],
        )

    def correct_first(slot, projected):
        for ri, p, _, there in blocks():
            correct_with(term1, split1, slot, slice(ri * part, (ri + 1) * part), there, projected)

    sweep(1, start_split, 2 * part, apply_first, correct_first)

    def images(order, source, slot, projected):
        for ri, p, here, there in blocks():
            sign = TIME_STEP / order if ri else -TIME_STEP / order
            pot = (pots[slot] + (3.0 + pulse_field(slot, p))) * sign
            yield [
                (there, cols, pot[:, cols] * v - (0.5 * sign) * around + projected[here, cols])
                for cols, v, around in block_of(source, slot, here)
            ]

    def later(order, source, halves, target, target_split):
        def apply(slot, projected):
            for pieces in images(order, source, slot, projected):
                put(target, target_split, slot, pieces)

        def correct(slot, projected):
            for _, _, here, there in blocks():
                correct_with(target, target_split, slot, here, there, projected)

        sweep(order, halves, 4 * part, apply, correct)

    later(2, term1, split1, term2, split2)
    later(3, term2, split2, term3, split1)

    def apply_last(slot, projected):
        at = slot - HALO
        for pieces in images(TERMS, term3, slot, projected):
            sums = []
            for there, cols, image in pieces:
                begun = (there.start // (2 * part)) * part
                terms = term1[slot, there, cols] + term2[slot, there, cols] + term3[slot, there, cols]
                sums.append(start[slot, begun : begun + part, cols] + terms + image)
            for (there, cols, _), value in zip(pieces, sums):
                total[at, there, cols] = value

    def correct_last(slot, projected):
        at = slot - HALO
        for _, _, here, there in blocks():
            total[at, there] += projected[here]

    sweep(TERMS, split1, 4 * part, apply_last, correct_last)

    shares = jnp.zeros((4 * part, 128), F32)
    for slot in range(GROUP):
        position = (plane_of(slot + HALO).astype(F32) + 0.5) / slabs
        squares = jnp.zeros((4 * part, 128), F32)
        for j in range(8):
            v = total[slot, :, columns(j)]
            squares += v * v
        shares += position * squares
    for p in range(2):
        rows = slice(p * part, (p + 1) * part)
        value = jnp.sum(shares[rows] + shares[slice((2 + p) * part, (3 + p) * part)])
        moment[p : p + 1, :] = jnp.full((1, 128), value, F32)
    for number, out in enumerate(outs):
        yy = y if number // 2 == 0 else 1 - y
        xx = x if number % 2 == 0 else 1 - x
        for core in range(2):
            for ri in range(2):
                start_row = pl.multiple_of((2 * ri + yy) * part, part)
                at = (2 * core + ri) * part
                out[at : at + part, :] = total[2 * xx + core, pl.ds(start_row, part), :]


def unpack_kernel(*refs):
    pieces, out, rows, halves = refs[:8], refs[8], refs[9], refs[10:]
    y, _, x, c = place()
    cells, channels = out.shape
    half = channels // 2
    part = half // 8
    for number, piece in enumerate(pieces):
        yy = y if number // 4 == 0 else 1 - y
        xx = x if number // 2 % 2 == 0 else 1 - x
        cc = c if number % 2 == 0 else 1 - c
        at = pl.multiple_of((4 * yy + 2 * xx + cc) * part, part)
        for ri in range(2):
            start = pl.multiple_of((2 * c + ri) * part, part)
            rows[pl.ds(at + ri * half, part), :] = piece[pl.ds(start, part), :]
    lanes = cells // 8
    for j in range(8):
        for ri in range(2):
            block = rows[ri * half : (ri + 1) * half, j * lanes : (j + 1) * lanes].T
            halves[ri][pl.ds(j, lanes, stride=8), :] = block
    for ri in range(2):
        out[:, ri * half : (ri + 1) * half] = halves[ri][...]


VMEM = pl.BlockSpec(memory_space=pltpu.VMEM)
SMEM = pl.BlockSpec(memory_space=pltpu.SMEM)
BOTH = ("pulse", "grid")


def local(slabs, orbitals, potential, pulse, projectors, couplings, sphere_points, atom_count):
    _, nx, ny, channels = orbitals.shape
    cells = nx * ny
    atoms, k, size = projectors.shape
    part = channels // 16
    y, g = lax.axis_index("pulse"), lax.axis_index("grid")
    quads = slabs // GROUP
    quad = g // GROUP

    def permute(value, target):
        pairs = []
        for p in range(2):
            for s in range(slabs):
                to = target(p, s)
                if to is not None:
                    pairs.append((p * slabs + s, to[0] * slabs + to[1]))
        return lax.ppermute(value, BOTH, pairs)

    def swap_core(value):
        return permute(value, lambda p, s: (p, s ^ 1))

    def shift(value, by):
        return permute(value, lambda p, s: (p, s + by) if 0 <= s + by < slabs else None)

    bundle = jax.ShapeDtypeStruct((5 * channels // 16, cells), F32)
    near, far = pl.pallas_call(
        pack_kernel,
        out_shape=(bundle, bundle),
        in_specs=[VMEM] * 5 + [SMEM],
        out_specs=[VMEM] * 2,
        scratch_shapes=[pltpu.VMEM((cells, channels // 2), F32), pltpu.VMEM((channels // 2, cells), F32)],
        compiler_params=pltpu.CompilerParams(vmem_limit_bytes=8 * 2**20),
        name="pack",
    )(orbitals.reshape(cells, channels), potential.reshape(nx, ny), projectors, couplings.T, sphere_points, atom_count)
    beside = permute(far, lambda p, s: (p, s ^ 2))
    below1, above1 = shift(near, GROUP), shift(near, -GROUP)
    heavy = pl.pallas_call(
        rest_kernel,
        out_shape=jax.ShapeDtypeStruct((32, cells), F32),
        in_specs=[VMEM] * 3,
        out_specs=VMEM,
        compiler_params=pltpu.CompilerParams(vmem_limit_bytes=4 * 2**20),
        name="rest",
    )(projectors, sphere_points, near)
    below2, above2 = shift(beside, GROUP), shift(beside, -GROUP)
    near_mate, pulse_sent = lax.optimization_barrier((swap_core(near), pulse))
    other_pulse = permute(pulse_sent, lambda p, s: (1 - p, s))
    above1, below1, other_pulse = lax.optimization_barrier((above1, below1, other_pulse))
    order = []
    for piece in (below1, below2, near, beside, above1, above2):
        order += [piece, near_mate if piece is near else swap_core(piece)]

    edge = max(slabs // 8, 1)
    shared_heavy = not (edge == 2 and quads >= 4)
    if shared_heavy:
        everywhere = lax.all_gather(heavy, "grid")
        blank = jnp.zeros((HALO - 1,) + heavy.shape, F32)
        padded = jnp.concatenate([blank, everywhere, blank])
        heavies = [lax.dynamic_slice_in_dim(padded, quad * GROUP, SLOTS - 2)]
        stores = SLOTS - 2
    else:
        crowded = (0, 1, slabs - 2, slabs - 1)
        x = (g // 2) % 2
        own = ((quad == 0) & (x == 0)) | ((quad == quads - 1) & (x == 1))
        inner = {1: GROUP, slabs - 2: -GROUP}
        across = permute(heavy, lambda p, s: (p, s ^ 2) if s in crowded else None)
        along = permute(heavy, lambda p, s: (p, s + inner[s]) if s in inner else None)
        over = permute(heavy, lambda p, s: (p, (s + inner[s]) ^ 2) if s in inner else None)
        held = jnp.where(own, heavy, across + along + over)
        heavies = [held, swap_core(held)]
        stores = 2

    outs = pl.pallas_call(
        functools.partial(evolve_kernel, slabs, shared_heavy),
        out_shape=[jax.ShapeDtypeStruct((4 * part, cells), F32)] * 4 + [jax.ShapeDtypeStruct((2, 128), F32)],
        in_specs=[SMEM] * 2 + [VMEM] * (12 + len(heavies)),
        out_specs=[VMEM] * 5,
        scratch_shapes=[pltpu.VMEM((SLOTS, 2 * part, cells), F32)]
        + [pltpu.VMEM((SLOTS, 4 * part, cells), F32)] * 3
        + [pltpu.VMEM((SLOTS, 4 * part, cells), BF16)]
        + [pltpu.VMEM((SLOTS, 8 * part, cells), BF16)] * 2
        + [
            pltpu.VMEM((GROUP, 4 * part, cells), F32),
            pltpu.VMEM((SLOTS, 3 * LIGHT * k, cells), BF16),
            pltpu.VMEM((stores, 3 * atoms * k, cells), BF16),
            pltpu.VMEM((SLOTS, 1, cells), F32),
            pltpu.VMEM((SLOTS, 1, 128), F32),
            pltpu.VMEM((2, 2, 4 * part, 3 * LIGHT * k), BF16),
        ],
        compiler_params=pltpu.CompilerParams(vmem_limit_bytes=(28 if not shared_heavy else 40) * 2**20),
        name="evolve",
    )(pulse, other_pulse, *order, *heavies)
    moment = outs[4]
    finals = [
        outs[0],
        permute(outs[1], lambda p, s: (p, s ^ 2)),
        permute(outs[2], lambda p, s: (1 - p, s)),
        permute(outs[3], lambda p, s: (1 - p, s ^ 2)),
    ]
    devices = 2 * slabs
    shares = jnp.broadcast_to(jnp.concatenate([moment[0], moment[1]])[None, None, :], (devices, 1, 256))
    shares = lax.all_to_all(shares, BOTH, 0, 0)
    *finals, shares = lax.optimization_barrier((*finals, shares))
    pieces = []
    for piece in finals:
        pieces += [piece, swap_core(piece)]
    plane = pl.pallas_call(
        unpack_kernel,
        out_shape=jax.ShapeDtypeStruct((cells, channels), F32),
        in_specs=[VMEM] * 8,
        out_specs=VMEM,
        scratch_shapes=[pltpu.VMEM((channels, cells), F32)] + [pltpu.VMEM((cells, channels // 2), F32)] * 2,
        compiler_params=pltpu.CompilerParams(vmem_limit_bytes=16 * 2**20),
        name="unpack",
    )(*pieces)

    total = jnp.where(y == 0, jnp.sum(shares[:, 0, 0]), jnp.sum(shares[:, 0, 128]))
    dipole = total / (slabs * cells * (channels // 2))
    return plane.reshape(orbitals.shape), dipole.reshape(1)


def solution(mesh):
    placed = (
        P("grid", None, None, None),
        P("grid", None, None),
        P("pulse"),
        P("grid", None, None),
        P("grid", None),
        P("grid", None),
        P("grid"),
    )
    return jax.shard_map(
        functools.partial(local, mesh.shape["grid"]),
        mesh=mesh,
        in_specs=placed,
        out_specs=(P(("pulse", "grid"), None, None, None), P("pulse")),
        check_vma=False,
    )
```

```python
import functools

import jax
import jax.numpy as jnp
from jax import lax
from jax.experimental import pallas as pl
from jax.experimental.pallas import tpu as pltpu
from jax.sharding import PartitionSpec as P


TERMS = 4
TIME_STEP = 0.1
GROUP = 4
HALO = TERMS
SLOTS = GROUP + 2 * HALO
LIGHT = 4
F32 = jnp.float32
BF16 = jnp.bfloat16
NT = (((1,), (1,)), ((), ()))
NN = (((1,), (0,)), ((), ()))


def iota(shape, dim):
    return lax.broadcasted_iota(jnp.int32, shape, dim)


def split(value):
    high = value.astype(BF16)
    return high, (value - high.astype(F32)).astype(BF16)


def place():
    y, g = lax.axis_index("pulse"), lax.axis_index("grid")
    return y, g // GROUP, (g // 2) % 2, g % 2


def pack_kernel(orb, pot, proj, coup, points, count, near, far, packed, rows):
    y, _, x, _ = place()
    cells, channels = orb.shape
    lanes = cells // 8
    half = channels // 2
    first = iota((lanes, half), 1) < half // 2
    for j in range(8):
        chunk = slice(j * lanes, (j + 1) * lanes)
        re, im = orb[chunk, :half], orb[chunk, half:]
        low = jnp.where(first, re, pltpu.roll(im, half // 2, 1))
        high = jnp.where(first, pltpu.roll(re, half // 2, 1), im)
        packed[chunk, :] = jnp.where(y == 0, low, high)
    for j in range(8):
        rows[:, j * lanes : (j + 1) * lanes] = packed[pl.ds(j, lanes, stride=8), :].T
    part = half // 8
    for out, xx in ((near, x), (far, 1 - x)):
        for c in range(2):
            start = pl.multiple_of((2 * xx + c) * part, part)
            out[c * 2 * part : c * 2 * part + part, :] = rows[pl.ds(start, part), :]
            out[c * 2 * part + part : (c + 1) * 2 * part, :] = rows[pl.ds(start + half // 2, part), :]
    nx, ny = pot.shape
    yh = ny // 8
    col = iota((ny, cells), 1)
    pick = (iota((ny, cells), 0) == (col % lanes) % yh * 8 + col // lanes).astype(F32)
    spread = lax.dot_general(pot[...], pick, NN, precision=lax.Precision.HIGHEST, preferred_element_type=F32)
    keep = iota((nx, cells), 0) == (iota((nx, cells), 1) % lanes) // yh
    pot_row = jnp.sum(jnp.where(keep, spread, 0.0), axis=0, keepdims=True)
    k, atoms = coup.shape
    pick = (iota((atoms, atoms * k), 0) == iota((atoms, atoms * k), 1) // k).astype(F32)
    spread = lax.dot_general(coup[...], pick, NN, precision=lax.Precision.HIGHEST, preferred_element_type=F32)
    column = iota((k, atoms * k), 1)
    keep = (iota((k, atoms * k), 0) == column % k) & (column // k < count[0])
    weight_row = jnp.sum(jnp.where(keep, spread, 0.0), axis=0, keepdims=True)
    size = points.shape[1]
    base = 4 * part
    for out in (near, far):
        for a in range(LIGHT):
            out[base : base + k, a * size : (a + 1) * size] = proj[a].astype(F32)
            out[base + k : base + k + 1, a * size : (a + 1) * size] = points[a : a + 1, :].astype(F32)
        out[base + k + 1 : base + k + 2, :] = pot_row
        out[base + k + 2 : base + k + 3, :] = jnp.zeros((1, cells), F32)
        out[base + k + 2 : base + k + 3, : atoms * k] = weight_row
        out[base + k + 3 : base + k + 8, :] = jnp.zeros((5, cells), F32)


def rest_kernel(proj, points, near, rest):
    atoms, k, size = proj.shape
    groups = atoms // LIGHT - 1
    for group in range(groups):
        for a in range(LIGHT):
            source = (group + 1) * LIGHT + a
            rest[group * k : (group + 1) * k, a * size : (a + 1) * size] = proj[source].astype(F32)
            rest[groups * k + group : groups * k + group + 1, a * size : (a + 1) * size] = (
                points[source : source + 1, :].astype(F32)
            )
    used = groups * (k + 1)
    spare = rest.shape[0] - used
    rest[used:, :] = near[near.shape[0] - spare :, :]


def matrix_of(proj, points, size):
    k = proj.shape[0]
    parts = []
    for a in range(LIGHT):
        values = proj[:, a * size : (a + 1) * size]
        cell = points[:, a * size : (a + 1) * size].astype(jnp.int32)
        low, lane = cell & 7, cell >> 3
        tall = jnp.concatenate([jnp.where(low == j, values, 0.0) for j in range(8)], axis=0).astype(BF16)
        hot = jnp.where(iota((128, size), 0) == lane, 1.0, 0.0).astype(BF16)
        sums = lax.dot_general(tall, hot, NT, preferred_element_type=F32)
        parts.append(jnp.concatenate([sums[j * k : (j + 1) * k, :] for j in range(8)], axis=1))
    return jnp.concatenate(parts, axis=0)


def roll_lanes(value, shift):
    return pltpu.roll(value, shift % value.shape[1], 1)


def evolve_kernel(slabs, shared_heavy, *refs):
    own_pulse, other_pulse = refs[:2]
    bundles = refs[2:14]
    heavies = refs[14:15] if shared_heavy else refs[14:16]
    refs = refs[14 + len(heavies) :]
    outs, moment = refs[:4], refs[4]
    start, term1, term2, term3, start_split, split1, split2, total, light, full, pots, weights, coming = refs[5:]
    y, quad, x, c = place()
    quads = slabs // GROUP
    part = start.shape[1] // 2
    cells = start.shape[2]
    k = 8
    size = cells // LIGHT
    base = 4 * part
    span = LIGHT * k
    edge = max(slabs // 8, 1)
    has_low, has_high = quad > 0, quad < quads - 1

    def plane_of(slot):
        return quad * GROUP + slot - HALO

    def pulse_field(slot, p):
        strength = jnp.where(y == p, own_pulse[0], other_pulse[0])
        position = (plane_of(slot).astype(F32) + 0.5) / slabs
        return strength * 4.0 * (position - 0.5)

    for number, bundle in enumerate(bundles):
        direction, xf, cf = number // 4, number // 2 % 2, number % 2
        slot = direction * GROUP + 2 * (x if xf == 0 else 1 - x) + (c if cf == 0 else 1 - c)
        rows = bundle[pl.ds(pl.multiple_of(c * 2 * part, 2 * part), 2 * part), :]
        start[slot] = rows
        high, low = split(rows)
        start_split[slot, : 2 * part] = high
        start_split[slot, 2 * part :] = low
        pot_row = bundle[base + k + 1 : base + k + 2, :] + 3.0
        for p in range(2):
            pots[slot, p] = pot_row + pulse_field(slot, p)
        weights[slot] = bundle[base + k + 2 : base + k + 3, : 4 * span]

        def build(bundle=bundle, slot=slot):
            high, low = split(matrix_of(bundle[base : base + k, :], bundle[base + k : base + k + 1, :], size))
            light[slot, :span] = high
            light[slot, span : 2 * span] = low
            light[slot, 2 * span :] = high

        if direction == 1:
            build()
        else:
            pl.when((has_low if direction == 0 else has_high) & (slot > 0) & (slot < SLOTS - 1))(build)

    def is_heavy(slot):
        plane = plane_of(slot)
        return (plane < edge) | (plane >= slabs - edge)

    wide = 4 * span

    def build_full(store, source, slot):
        for part_of in range(3):
            full[store, part_of * wide : part_of * wide + span] = light[slot, part_of * span : (part_of + 1) * span]
        for group in range(3):
            high, low = split(matrix_of(source(group * k, k), source(3 * k + group, 1), size))
            for part_of, value in enumerate((high, low, high)):
                at = part_of * wide + (group + 1) * span
                full[store, at : at + span] = value

    if shared_heavy:

        def store_of(slot):
            return slot - 1

        for slot in range(1, SLOTS - 1):
            exists = (plane_of(slot) >= 0) & (plane_of(slot) < slabs)

            @pl.when(exists & is_heavy(slot))
            def _(slot=slot):
                build_full(slot - 1, lambda at, n: heavies[0][slot - 1, at : at + n, :], slot)
    else:
        ends = (quad == 0) | (quad == quads - 1)
        beside = (quad == 1) | (quad == quads - 2)
        low_end = quad <= 1
        first_slot = jnp.where(low_end, HALO, HALO + 2)

        def store_of(slot):
            return jnp.where(ends, slot - first_slot, 0)

        @pl.when(ends)
        def _():
            for cf in range(2):
                core = c if cf == 0 else 1 - c
                build_full(core, lambda at, n, cf=cf: heavies[cf][at : at + n, :], first_slot + core)

        @pl.when(beside)
        def _():
            mine = (c == 1) == low_end
            lone = jnp.where(low_end, 1, SLOTS - 2)
            build_full(0, lambda at, n: jnp.where(mine, heavies[0][at : at + n, :], heavies[1][at : at + n, :]), lone)

    for missing, slot in ((jnp.logical_not(has_low), HALO - 1), (jnp.logical_not(has_high), HALO + GROUP)):

        @pl.when(missing)
        def _(slot=slot):
            for term in (term1, term2, term3):
                term[slot] = jnp.zeros(term.shape[1:], F32)

    def coefficients(halves, matrix, weight, count, width, factor):
        r = lax.dot_general(halves, matrix, NT, preferred_element_type=F32)
        coeffs = r[:count, :width] + r[count:, :width] + r[:count, width:]
        sign = jnp.where(iota((count, width), 0) < count // 2, -factor, factor)
        high, low = split(coeffs * weight * sign)
        return jnp.concatenate([high, high, low], axis=1)

    lane = iota((1, 128), 1)
    groups_y = 4
    wrap_up, wrap_down = lane % groups_y == groups_y - 1, lane % groups_y == 0

    def columns(j):
        return slice(j * 128, (j + 1) * 128)

    def block_of(field, slot, rows):
        values = [field[slot, rows, columns(j)] for j in range(8)]
        beyond = [field[slot - 1, rows, columns(j)] + field[slot + 1, rows, columns(j)] for j in range(8)]
        for j, v in enumerate(values):
            around = beyond[j] + (roll_lanes(v, groups_y) + roll_lanes(v, -groups_y))
            w = values[(j + 1) % 8]
            around += w if j < 7 else jnp.where(wrap_up, roll_lanes(w, groups_y - 1), roll_lanes(w, -1))
            w = values[(j - 1) % 8]
            around += w if j > 0 else jnp.where(wrap_down, roll_lanes(w, 1 - groups_y), roll_lanes(w, 1))
            yield columns(j), v, around

    def put(term, halves, slot, pieces):
        halved = [split(value) for _, _, value in pieces]
        for (rows, cols, value), (high, low) in zip(pieces, halved):
            term[slot, rows, cols] = value
            halves[slot, rows, cols] = high
            halves[slot, slice(4 * part + rows.start, 4 * part + rows.stop), cols] = low

    def bounds(order):
        reach = TERMS - order
        low = jnp.where(has_low, HALO - reach, HALO)
        high = jnp.where(has_high, HALO + GROUP + reach, HALO + GROUP)
        return low, high

    def sweep(order, halves, count, apply, correct):
        factor = TIME_STEP / order
        low, high = bounds(order)

        begin = jnp.where(has_high, low, low - low % 2)
        number = (high - begin + 1) // 2

        def pair(i):
            return jnp.clip(begin + 2 * i, low, high - 1), jnp.minimum(begin + 2 * i + 1, high - 1)

        def ahead(i):
            for side, slot in enumerate(pair(i)):
                coming[i % 2, side, :count] = coefficients(
                    halves[slot], light[slot, : 2 * span, :], weights[slot][:, :span], count, span, factor
                )

        def whole(slot, beyond):
            store = store_of(slot)
            weight = jnp.where(iota((1, wide), 1) < span, 0.0, weights[slot]) if beyond else weights[slot]
            right = coefficients(halves[slot], full[store, : 2 * wide, :], weight, count, wide, factor)
            return lax.dot_general(right, full[store], NN, preferred_element_type=F32)

        def body(i, carry):
            slots = pair(i)
            distinct = slots[0] != slots[1]
            both = is_heavy(slots[0]) & is_heavy(slots[1]) & distinct

            @pl.when(jnp.logical_not(both))
            def _():
                ahead(i + 1)
                for side, slot in enumerate(slots):
                    apply(
                        slot,
                        lax.dot_general(coming[i % 2, side, :count], light[slot], NN, preferred_element_type=F32),
                    )

            @pl.when(both)
            def _():
                ahead(i + 1)
                for slot in slots:
                    apply(slot, whole(slot, False))

            @pl.when((is_heavy(slots[0]) | is_heavy(slots[1])) & jnp.logical_not(both))
            def _():
                for side, slot in enumerate(slots):

                    @pl.when(is_heavy(slot) & (distinct | (side == 0)))
                    def _(slot=slot):
                        correct(slot, whole(slot, True))

            return carry

        ahead(0)
        lax.fori_loop(0, number, body, 0)

    def blocks():
        for ri in range(2):
            for p in range(2):
                here, there = (2 * ri + p) * part, (2 * (1 - ri) + p) * part
                yield ri, p, slice(here, here + part), slice(there, there + part)

    def apply_first(slot, projected):
        for ri in range(2):
            sign = TIME_STEP if ri else -TIME_STEP
            rows = slice(ri * part, (ri + 1) * part)
            images = [
                (cols, projected[rows, cols] - (0.5 * sign) * around, v)
                for cols, v, around in block_of(start, slot, rows)
            ]
            for p in range(2):
                there = (2 * (1 - ri) + p) * part
                there = slice(there, there + part)
                pot = pots[slot, p] * sign
                put(term1, split1, slot, [(there, cols, image + pot[:, cols] * v) for cols, image, v in images])

    def correct_with(term, halves, slot, rows, there, projected):
        put(
            term, halves, slot,
            [(there, columns(j), term[slot, there, columns(j)] + projected[rows, columns(j)]) for j in range(8)],
        )

    def correct_first(slot, projected):
        for ri, p, _, there in blocks():
            correct_with(term1, split1, slot, slice(ri * part, (ri + 1) * part), there, projected)

    sweep(1, start_split, 2 * part, apply_first, correct_first)

    def images(order, source, slot, projected):
        for ri, p, here, there in blocks():
            sign = TIME_STEP / order if ri else -TIME_STEP / order
            pot = pots[slot, p] * sign
            yield [
                (there, cols, pot[:, cols] * v - (0.5 * sign) * around + projected[here, cols])
                for cols, v, around in block_of(source, slot, here)
            ]

    def later(order, source, halves, target, target_split):
        def apply(slot, projected):
            for pieces in images(order, source, slot, projected):
                put(target, target_split, slot, pieces)

        def correct(slot, projected):
            for _, _, here, there in blocks():
                correct_with(target, target_split, slot, here, there, projected)

        sweep(order, halves, 4 * part, apply, correct)

    later(2, term1, split1, term2, split2)
    later(3, term2, split2, term3, split1)

    def apply_last(slot, projected):
        at = slot - HALO
        for pieces in images(TERMS, term3, slot, projected):
            sums = []
            for there, cols, image in pieces:
                begun = (there.start // (2 * part)) * part
                terms = term1[slot, there, cols] + term2[slot, there, cols] + term3[slot, there, cols]
                sums.append(start[slot, begun : begun + part, cols] + terms + image)
            for (there, cols, _), value in zip(pieces, sums):
                total[at, there, cols] = value

    def correct_last(slot, projected):
        at = slot - HALO
        for _, _, here, there in blocks():
            total[at, there] += projected[here]

    sweep(TERMS, split1, 4 * part, apply_last, correct_last)

    shares = jnp.zeros((4 * part, 128), F32)
    for slot in range(GROUP):
        position = (plane_of(slot + HALO).astype(F32) + 0.5) / slabs
        squares = jnp.zeros((4 * part, 128), F32)
        for j in range(8):
            v = total[slot, :, columns(j)]
            squares += v * v
        shares += position * squares
    for p in range(2):
        rows = slice(p * part, (p + 1) * part)
        value = jnp.sum(shares[rows] + shares[slice((2 + p) * part, (3 + p) * part)])
        moment[p : p + 1, :] = jnp.full((1, 128), value, F32)
    for number, out in enumerate(outs):
        yy = y if number // 2 == 0 else 1 - y
        xx = x if number % 2 == 0 else 1 - x
        for core in range(2):
            for ri in range(2):
                start_row = pl.multiple_of((2 * ri + yy) * part, part)
                at = (2 * core + ri) * part
                out[at : at + part, :] = total[2 * xx + core, pl.ds(start_row, part), :]


def unpack_kernel(*refs):
    pieces, out, rows, halves = refs[:8], refs[8], refs[9], refs[10:]
    y, _, x, c = place()
    cells, channels = out.shape
    half = channels // 2
    part = half // 8
    for number, piece in enumerate(pieces):
        yy = y if number // 4 == 0 else 1 - y
        xx = x if number // 2 % 2 == 0 else 1 - x
        cc = c if number % 2 == 0 else 1 - c
        at = pl.multiple_of((4 * yy + 2 * xx + cc) * part, part)
        for ri in range(2):
            start = pl.multiple_of((2 * c + ri) * part, part)
            rows[pl.ds(at + ri * half, part), :] = piece[pl.ds(start, part), :]
    lanes = cells // 8
    for j in range(8):
        for ri in range(2):
            block = rows[ri * half : (ri + 1) * half, j * lanes : (j + 1) * lanes].T
            halves[ri][pl.ds(j, lanes, stride=8), :] = block
    for ri in range(2):
        out[:, ri * half : (ri + 1) * half] = halves[ri][...]


VMEM = pl.BlockSpec(memory_space=pltpu.VMEM)
SMEM = pl.BlockSpec(memory_space=pltpu.SMEM)
BOTH = ("pulse", "grid")


def local(slabs, orbitals, potential, pulse, projectors, couplings, sphere_points, atom_count):
    _, nx, ny, channels = orbitals.shape
    cells = nx * ny
    atoms, k, size = projectors.shape
    part = channels // 16
    y, g = lax.axis_index("pulse"), lax.axis_index("grid")
    quads = slabs // GROUP
    quad = g // GROUP

    def permute(value, target):
        pairs = []
        for p in range(2):
            for s in range(slabs):
                to = target(p, s)
                if to is not None:
                    pairs.append((p * slabs + s, to[0] * slabs + to[1]))
        return lax.ppermute(value, BOTH, pairs)

    def swap_core(value):
        return permute(value, lambda p, s: (p, s ^ 1))

    def shift(value, by):
        return permute(value, lambda p, s: (p, s + by) if 0 <= s + by < slabs else None)

    bundle = jax.ShapeDtypeStruct((5 * channels // 16, cells), F32)
    near, far = pl.pallas_call(
        pack_kernel,
        out_shape=(bundle, bundle),
        in_specs=[VMEM] * 5 + [SMEM],
        out_specs=[VMEM] * 2,
        scratch_shapes=[pltpu.VMEM((cells, channels // 2), F32), pltpu.VMEM((channels // 2, cells), F32)],
        compiler_params=pltpu.CompilerParams(vmem_limit_bytes=8 * 2**20),
        name="pack",
    )(orbitals.reshape(cells, channels), potential.reshape(nx, ny), projectors, couplings.T, sphere_points, atom_count)
    beside = permute(far, lambda p, s: (p, s ^ 2))
    below1, above1 = shift(near, GROUP), shift(near, -GROUP)
    heavy = pl.pallas_call(
        rest_kernel,
        out_shape=jax.ShapeDtypeStruct((32, cells), F32),
        in_specs=[VMEM] * 3,
        out_specs=VMEM,
        compiler_params=pltpu.CompilerParams(vmem_limit_bytes=4 * 2**20),
        name="rest",
    )(projectors, sphere_points, near)
    below2, above2 = shift(beside, GROUP), shift(beside, -GROUP)
    near_mate, pulse_sent = lax.optimization_barrier((swap_core(near), pulse))
    other_pulse = permute(pulse_sent, lambda p, s: (1 - p, s))
    above1, below1, other_pulse = lax.optimization_barrier((above1, below1, other_pulse))
    order = []
    for piece in (below1, below2, near, beside, above1, above2):
        order += [piece, near_mate if piece is near else swap_core(piece)]

    edge = max(slabs // 8, 1)
    shared_heavy = not (edge == 2 and quads >= 4)
    if shared_heavy:
        everywhere = lax.all_gather(heavy, "grid")
        blank = jnp.zeros((HALO - 1,) + heavy.shape, F32)
        padded = jnp.concatenate([blank, everywhere, blank])
        heavies = [lax.dynamic_slice_in_dim(padded, quad * GROUP, SLOTS - 2)]
        stores = SLOTS - 2
    else:
        crowded = (0, 1, slabs - 2, slabs - 1)
        x = (g // 2) % 2
        own = ((quad == 0) & (x == 0)) | ((quad == quads - 1) & (x == 1))
        inner = {1: GROUP, slabs - 2: -GROUP}
        across = permute(heavy, lambda p, s: (p, s ^ 2) if s in crowded else None)
        along = permute(heavy, lambda p, s: (p, s + inner[s]) if s in inner else None)
        over = permute(heavy, lambda p, s: (p, (s + inner[s]) ^ 2) if s in inner else None)
        held = jnp.where(own, heavy, across + along + over)
        heavies = [held, swap_core(held)]
        stores = 2

    outs = pl.pallas_call(
        functools.partial(evolve_kernel, slabs, shared_heavy),
        out_shape=[jax.ShapeDtypeStruct((4 * part, cells), F32)] * 4 + [jax.ShapeDtypeStruct((2, 128), F32)],
        in_specs=[SMEM] * 2 + [VMEM] * (12 + len(heavies)),
        out_specs=[VMEM] * 5,
        scratch_shapes=[pltpu.VMEM((SLOTS, 2 * part, cells), F32)]
        + [pltpu.VMEM((SLOTS, 4 * part, cells), F32)] * 3
        + [pltpu.VMEM((SLOTS, 4 * part, cells), BF16)]
        + [pltpu.VMEM((SLOTS, 8 * part, cells), BF16)] * 2
        + [
            pltpu.VMEM((GROUP, 4 * part, cells), F32),
            pltpu.VMEM((SLOTS, 3 * LIGHT * k, cells), BF16),
            pltpu.VMEM((stores, 3 * atoms * k, cells), BF16),
            pltpu.VMEM((SLOTS, 2, 1, cells), F32),
            pltpu.VMEM((SLOTS, 1, 128), F32),
            pltpu.VMEM((2, 2, 4 * part, 3 * LIGHT * k), BF16),
        ],
        compiler_params=pltpu.CompilerParams(vmem_limit_bytes=(28 if not shared_heavy else 40) * 2**20),
        name="evolve",
    )(pulse, other_pulse, *order, *heavies)
    moment = outs[4]
    finals = [
        outs[0],
        permute(outs[1], lambda p, s: (p, s ^ 2)),
        permute(outs[2], lambda p, s: (1 - p, s)),
        permute(outs[3], lambda p, s: (1 - p, s ^ 2)),
    ]
    devices = 2 * slabs
    shares = jnp.broadcast_to(jnp.concatenate([moment[0], moment[1]])[None, None, :], (devices, 1, 256))
    shares = lax.all_to_all(shares, BOTH, 0, 0)
    *finals, shares = lax.optimization_barrier((*finals, shares))
    pieces = []
    for piece in finals:
        pieces += [piece, swap_core(piece)]
    plane = pl.pallas_call(
        unpack_kernel,
        out_shape=jax.ShapeDtypeStruct((cells, channels), F32),
        in_specs=[VMEM] * 8,
        out_specs=VMEM,
        scratch_shapes=[pltpu.VMEM((channels, cells), F32)] + [pltpu.VMEM((cells, channels // 2), F32)] * 2,
        compiler_params=pltpu.CompilerParams(vmem_limit_bytes=16 * 2**20),
        name="unpack",
    )(*pieces)

    total = jnp.where(y == 0, jnp.sum(shares[:, 0, 0]), jnp.sum(shares[:, 0, 128]))
    dipole = total / (slabs * cells * (channels // 2))
    return plane.reshape(orbitals.shape), dipole.reshape(1)


def solution(mesh):
    placed = (
        P("grid", None, None, None),
        P("grid", None, None),
        P("pulse"),
        P("grid", None, None),
        P("grid", None),
        P("grid", None),
        P("grid"),
    )
    return jax.shard_map(
        functools.partial(local, mesh.shape["grid"]),
        mesh=mesh,
        in_specs=placed,
        out_specs=(P(("pulse", "grid"), None, None, None), P("pulse")),
        check_vma=False,
    )
```

```python
import functools

import jax
import jax.numpy as jnp
from jax import lax
from jax.experimental import pallas as pl
from jax.experimental.pallas import tpu as pltpu
from jax.sharding import PartitionSpec as P


TERMS = 4
TIME_STEP = 0.1
GROUP = 4
HALO = TERMS
SLOTS = GROUP + 2 * HALO
LIGHT = 4
F32 = jnp.float32
BF16 = jnp.bfloat16
NT = (((1,), (1,)), ((), ()))
NN = (((1,), (0,)), ((), ()))


def iota(shape, dim):
    return lax.broadcasted_iota(jnp.int32, shape, dim)


def split(value):
    high = value.astype(BF16)
    return high, (value - high.astype(F32)).astype(BF16)


def place():
    y, g = lax.axis_index("pulse"), lax.axis_index("grid")
    return y, g // GROUP, (g // 2) % 2, g % 2


def pack_kernel(orb, pot, proj, coup, points, count, near, far, packed, rows):
    y, _, x, _ = place()
    cells, channels = orb.shape
    lanes = cells // 8
    half = channels // 2
    first = iota((lanes, half), 1) < half // 2
    for j in range(8):
        chunk = slice(j * lanes, (j + 1) * lanes)
        re, im = orb[chunk, :half], orb[chunk, half:]
        low = jnp.where(first, re, pltpu.roll(im, half // 2, 1))
        high = jnp.where(first, pltpu.roll(re, half // 2, 1), im)
        packed[chunk, :] = jnp.where(y == 0, low, high)
    for j in range(8):
        rows[:, j * lanes : (j + 1) * lanes] = packed[pl.ds(j, lanes, stride=8), :].T
    part = half // 8
    for out, xx in ((near, x), (far, 1 - x)):
        for c in range(2):
            start = pl.multiple_of((2 * xx + c) * part, part)
            out[c * 2 * part : c * 2 * part + part, :] = rows[pl.ds(start, part), :]
            out[c * 2 * part + part : (c + 1) * 2 * part, :] = rows[pl.ds(start + half // 2, part), :]
    nx, ny = pot.shape
    yh = ny // 8
    col = iota((ny, cells), 1)
    pick = (iota((ny, cells), 0) == (col % lanes) % yh * 8 + col // lanes).astype(F32)
    spread = lax.dot_general(pot[...], pick, NN, precision=lax.Precision.HIGHEST, preferred_element_type=F32)
    keep = iota((nx, cells), 0) == (iota((nx, cells), 1) % lanes) // yh
    pot_row = jnp.sum(jnp.where(keep, spread, 0.0), axis=0, keepdims=True)
    k, atoms = coup.shape
    pick = (iota((atoms, atoms * k), 0) == iota((atoms, atoms * k), 1) // k).astype(F32)
    spread = lax.dot_general(coup[...], pick, NN, precision=lax.Precision.HIGHEST, preferred_element_type=F32)
    column = iota((k, atoms * k), 1)
    keep = (iota((k, atoms * k), 0) == column % k) & (column // k < count[0])
    weight_row = jnp.sum(jnp.where(keep, spread, 0.0), axis=0, keepdims=True)
    size = points.shape[1]
    base = 4 * part
    for out in (near, far):
        for a in range(LIGHT):
            out[base : base + k, a * size : (a + 1) * size] = proj[a].astype(F32)
            out[base + k : base + k + 1, a * size : (a + 1) * size] = points[a : a + 1, :].astype(F32)
        out[base + k + 1 : base + k + 2, :] = pot_row
        out[base + k + 2 : base + k + 3, :] = jnp.zeros((1, cells), F32)
        out[base + k + 2 : base + k + 3, : atoms * k] = weight_row
        out[base + k + 3 : base + k + 8, :] = jnp.zeros((5, cells), F32)


def rest_kernel(proj, points, near, rest):
    atoms, k, size = proj.shape
    groups = atoms // LIGHT - 1
    for group in range(groups):
        for a in range(LIGHT):
            source = (group + 1) * LIGHT + a
            rest[group * k : (group + 1) * k, a * size : (a + 1) * size] = proj[source].astype(F32)
            rest[groups * k + group : groups * k + group + 1, a * size : (a + 1) * size] = (
                points[source : source + 1, :].astype(F32)
            )
    used = groups * (k + 1)
    spare = rest.shape[0] - used
    rest[used:, :] = near[near.shape[0] - spare :, :]


def matrix_of(proj, points, size):
    k = proj.shape[0]
    parts = []
    for a in range(LIGHT):
        values = proj[:, a * size : (a + 1) * size]
        cell = points[:, a * size : (a + 1) * size].astype(jnp.int32)
        low, lane = cell & 7, cell >> 3
        tall = jnp.concatenate([jnp.where(low == j, values, 0.0) for j in range(8)], axis=0).astype(BF16)
        hot = jnp.where(iota((128, size), 0) == lane, 1.0, 0.0).astype(BF16)
        sums = lax.dot_general(tall, hot, NT, preferred_element_type=F32)
        parts.append(jnp.concatenate([sums[j * k : (j + 1) * k, :] for j in range(8)], axis=1))
    return jnp.concatenate(parts, axis=0)


def roll_lanes(value, shift):
    return pltpu.roll(value, shift % value.shape[1], 1)


def evolve_kernel(slabs, shared_heavy, *refs):
    own_pulse, other_pulse = refs[:2]
    bundles = refs[2:14]
    heavies = refs[14:15] if shared_heavy else refs[14:16]
    refs = refs[14 + len(heavies) :]
    outs, moment = refs[:4], refs[4]
    start, term1, term2, term3, start_split, split1, split2, total, light, full, pots, weights, coming = refs[5:]
    y, quad, x, c = place()
    quads = slabs // GROUP
    part = start.shape[1] // 2
    cells = start.shape[2]
    k = 8
    size = cells // LIGHT
    base = 4 * part
    span = LIGHT * k
    edge = max(slabs // 8, 1)
    has_low, has_high = quad > 0, quad < quads - 1

    for number, bundle in enumerate(bundles):
        direction, xf, cf = number // 4, number // 2 % 2, number % 2
        slot = direction * GROUP + 2 * (x if xf == 0 else 1 - x) + (c if cf == 0 else 1 - c)
        rows = bundle[pl.ds(pl.multiple_of(c * 2 * part, 2 * part), 2 * part), :]
        start[slot] = rows
        high, low = split(rows)
        start_split[slot, : 2 * part] = high
        start_split[slot, 2 * part :] = low
        pots[slot] = bundle[base + k + 1 : base + k + 2, :]
        weights[slot] = bundle[base + k + 2 : base + k + 3, : 4 * span]

        def build(bundle=bundle, slot=slot):
            high, low = split(matrix_of(bundle[base : base + k, :], bundle[base + k : base + k + 1, :], size))
            light[slot, :span] = high
            light[slot, span : 2 * span] = low
            light[slot, 2 * span :] = high

        if direction == 1:
            build()
        else:
            pl.when((has_low if direction == 0 else has_high) & (slot > 0) & (slot < SLOTS - 1))(build)

    def plane_of(slot):
        return quad * GROUP + slot - HALO

    def is_heavy(slot):
        plane = plane_of(slot)
        return (plane < edge) | (plane >= slabs - edge)

    wide = 4 * span

    def build_full(store, source, slot):
        for part_of in range(3):
            full[store, part_of * wide : part_of * wide + span] = light[slot, part_of * span : (part_of + 1) * span]
        for group in range(3):
            high, low = split(matrix_of(source(group * k, k), source(3 * k + group, 1), size))
            for part_of, value in enumerate((high, low, high)):
                at = part_of * wide + (group + 1) * span
                full[store, at : at + span] = value

    if shared_heavy:

        def store_of(slot):
            return slot - 1

        for slot in range(1, SLOTS - 1):
            exists = (plane_of(slot) >= 0) & (plane_of(slot) < slabs)

            @pl.when(exists & is_heavy(slot))
            def _(slot=slot):
                build_full(slot - 1, lambda at, n: heavies[0][slot - 1, at : at + n, :], slot)
    else:
        ends = (quad == 0) | (quad == quads - 1)
        beside = (quad == 1) | (quad == quads - 2)
        low_end = quad <= 1
        first_slot = jnp.where(low_end, HALO, HALO + 2)

        def store_of(slot):
            return jnp.where(ends, slot - first_slot, 0)

        @pl.when(ends)
        def _():
            for cf in range(2):
                core = c if cf == 0 else 1 - c
                build_full(core, lambda at, n, cf=cf: heavies[cf][at : at + n, :], first_slot + core)

        @pl.when(beside)
        def _():
            mine = (c == 1) == low_end
            lone = jnp.where(low_end, 1, SLOTS - 2)
            build_full(0, lambda at, n: jnp.where(mine, heavies[0][at : at + n, :], heavies[1][at : at + n, :]), lone)

    for missing, slot in ((jnp.logical_not(has_low), HALO - 1), (jnp.logical_not(has_high), HALO + GROUP)):

        @pl.when(missing)
        def _(slot=slot):
            for term in (term1, term2, term3):
                term[slot] = jnp.zeros(term.shape[1:], F32)

    def coefficients(halves, matrix, weight, count, width, factor):
        r = lax.dot_general(halves, matrix, NT, preferred_element_type=F32)
        coeffs = r[:count, :width] + r[count:, :width] + r[:count, width:]
        sign = jnp.where(iota((count, width), 0) < count // 2, -factor, factor)
        high, low = split(coeffs * weight * sign)
        return jnp.concatenate([high, high, low], axis=1)

    lane = iota((1, 128), 1)
    groups_y = 4
    wrap_up, wrap_down = lane % groups_y == groups_y - 1, lane % groups_y == 0

    def columns(j):
        return slice(j * 128, (j + 1) * 128)

    def block_of(field, slot, rows):
        values = [field[slot, rows, columns(j)] for j in range(8)]
        beyond = [field[slot - 1, rows, columns(j)] + field[slot + 1, rows, columns(j)] for j in range(8)]
        for j, v in enumerate(values):
            around = beyond[j] + (roll_lanes(v, groups_y) + roll_lanes(v, -groups_y))
            w = values[(j + 1) % 8]
            around += w if j < 7 else jnp.where(wrap_up, roll_lanes(w, groups_y - 1), roll_lanes(w, -1))
            w = values[(j - 1) % 8]
            around += w if j > 0 else jnp.where(wrap_down, roll_lanes(w, 1 - groups_y), roll_lanes(w, 1))
            yield columns(j), v, around

    def pulse_field(slot, p):
        strength = jnp.where(y == p, own_pulse[0], other_pulse[0])
        position = (plane_of(slot).astype(F32) + 0.5) / slabs
        return strength * 4.0 * (position - 0.5)

    def put(term, halves, slot, pieces):
        halved = [split(value) for _, _, value in pieces]
        for (rows, cols, value), (high, low) in zip(pieces, halved):
            term[slot, rows, cols] = value
            halves[slot, rows, cols] = high
            halves[slot, slice(4 * part + rows.start, 4 * part + rows.stop), cols] = low

    def bounds(order):
        reach = TERMS - order
        low = jnp.where(has_low, HALO - reach, HALO)
        high = jnp.where(has_high, HALO + GROUP + reach, HALO + GROUP)
        return low, high

    def sweep(order, halves, count, apply, correct):
        factor = TIME_STEP / order
        low, high = bounds(order)

        begin = jnp.where(has_high, low, low - low % 2)
        number = (high - begin + 1) // 2

        def pair(i):
            return jnp.clip(begin + 2 * i, low, high - 1), jnp.minimum(begin + 2 * i + 1, high - 1)

        def ahead(i):
            for side, slot in enumerate(pair(i)):
                coming[i % 2, side, :count] = coefficients(
                    halves[slot], light[slot, : 2 * span, :], weights[slot][:, :span], count, span, factor
                )

        def whole(slot, beyond):
            store = store_of(slot)
            weight = jnp.where(iota((1, wide), 1) < span, 0.0, weights[slot]) if beyond else weights[slot]
            right = coefficients(halves[slot], full[store, : 2 * wide, :], weight, count, wide, factor)
            return lax.dot_general(right, full[store], NN, preferred_element_type=F32)

        def body(i, carry):
            slots = pair(i)
            distinct = slots[0] != slots[1]
            both = is_heavy(slots[0]) & is_heavy(slots[1]) & distinct

            @pl.when(jnp.logical_not(both))
            def _():
                ahead(i + 1)
                for side, slot in enumerate(slots):
                    apply(
                        slot,
                        lax.dot_general(coming[i % 2, side, :count], light[slot], NN, preferred_element_type=F32),
                    )

            @pl.when(both)
            def _():
                ahead(i + 1)
                for slot in slots:
                    apply(slot, whole(slot, False))

            for side, slot in enumerate(slots):

                @pl.when(is_heavy(slot) & jnp.logical_not(both) & (distinct | (side == 0)))
                def _(slot=slot):
                    correct(slot, whole(slot, True))

            return carry

        ahead(0)
        lax.fori_loop(0, number, body, 0)

    def blocks():
        for ri in range(2):
            for p in range(2):
                here, there = (2 * ri + p) * part, (2 * (1 - ri) + p) * part
                yield ri, p, slice(here, here + part), slice(there, there + part)

    def apply_first(slot, projected):
        for ri in range(2):
            sign = TIME_STEP if ri else -TIME_STEP
            rows = slice(ri * part, (ri + 1) * part)
            pot = (pots[slot] + 3.0) * sign
            images = [
                (cols, pot[:, cols] * v - (0.5 * sign) * around + projected[rows, cols], v)
                for cols, v, around in block_of(start, slot, rows)
            ]
            for p in range(2):
                there = (2 * (1 - ri) + p) * part
                field = pulse_field(slot, p) * sign
                there = slice(there, there + part)
                put(term1, split1, slot, [(there, cols, image + field * v) for cols, image, v in images])

    def correct_with(term, halves, slot, rows, there, projected):
        put(
            term, halves, slot,
            [(there, columns(j), term[slot, there, columns(j)] + projected[rows, columns(j)]) for j in range(8)],
        )

    def correct_first(slot, projected):
        for ri, p, _, there in blocks():
            correct_with(term1, split1, slot, slice(ri * part, (ri + 1) * part), there, projected)

    sweep(1, start_split, 2 * part, apply_first, correct_first)

    def images(order, source, slot, projected):
        for ri, p, here, there in blocks():
            sign = TIME_STEP / order if ri else -TIME_STEP / order
            pot = (pots[slot] + (3.0 + pulse_field(slot, p))) * sign
            yield [
                (there, cols, pot[:, cols] * v - (0.5 * sign) * around + projected[here, cols])
                for cols, v, around in block_of(source, slot, here)
            ]

    def later(order, source, halves, target, target_split):
        def apply(slot, projected):
            for pieces in images(order, source, slot, projected):
                put(target, target_split, slot, pieces)

        def correct(slot, projected):
            for _, _, here, there in blocks():
                correct_with(target, target_split, slot, here, there, projected)

        sweep(order, halves, 4 * part, apply, correct)

    later(2, term1, split1, term2, split2)
    later(3, term2, split2, term3, split1)

    def apply_last(slot, projected):
        at = slot - HALO
        for pieces in images(TERMS, term3, slot, projected):
            sums = []
            for there, cols, image in pieces:
                begun = (there.start // (2 * part)) * part
                terms = term1[slot, there, cols] + term2[slot, there, cols] + term3[slot, there, cols]
                sums.append(start[slot, begun : begun + part, cols] + terms + image)
            for (there, cols, _), value in zip(pieces, sums):
                total[at, there, cols] = value

    def correct_last(slot, projected):
        at = slot - HALO
        for _, _, here, there in blocks():
            total[at, there] += projected[here]

    sweep(TERMS, split1, 4 * part, apply_last, correct_last)

    shares = jnp.zeros((4 * part, 128), F32)
    for slot in range(GROUP):
        position = (plane_of(slot + HALO).astype(F32) + 0.5) / slabs
        squares = jnp.zeros((4 * part, 128), F32)
        for j in range(8):
            v = total[slot, :, columns(j)]
            squares += v * v
        shares += position * squares
    values = [
        jnp.sum(shares[p * part : (p + 1) * part] + shares[(2 + p) * part : (3 + p) * part]) for p in range(2)
    ]
    moment[...] = jnp.where(iota(moment.shape, 2) < 64, values[0], values[1])
    for number, out in enumerate(outs):
        yy = y if number // 2 == 0 else 1 - y
        xx = x if number % 2 == 0 else 1 - x
        for core in range(2):
            for ri in range(2):
                start_row = pl.multiple_of((2 * ri + yy) * part, part)
                at = (2 * core + ri) * part
                out[at : at + part, :] = total[2 * xx + core, pl.ds(start_row, part), :]


def unpack_kernel(*refs):
    pieces, out, rows, halves = refs[:8], refs[8], refs[9], refs[10:]
    y, _, x, c = place()
    cells, channels = out.shape
    half = channels // 2
    part = half // 8
    for number, piece in enumerate(pieces):
        yy = y if number // 4 == 0 else 1 - y
        xx = x if number // 2 % 2 == 0 else 1 - x
        cc = c if number % 2 == 0 else 1 - c
        at = pl.multiple_of((4 * yy + 2 * xx + cc) * part, part)
        for ri in range(2):
            start = pl.multiple_of((2 * c + ri) * part, part)
            rows[pl.ds(at + ri * half, part), :] = piece[pl.ds(start, part), :]
    lanes = cells // 8
    for j in range(8):
        for ri in range(2):
            block = rows[ri * half : (ri + 1) * half, j * lanes : (j + 1) * lanes].T
            halves[ri][pl.ds(j, lanes, stride=8), :] = block
    for ri in range(2):
        out[:, ri * half : (ri + 1) * half] = halves[ri][...]


VMEM = pl.BlockSpec(memory_space=pltpu.VMEM)
SMEM = pl.BlockSpec(memory_space=pltpu.SMEM)
BOTH = ("pulse", "grid")


def local(slabs, orbitals, potential, pulse, projectors, couplings, sphere_points, atom_count):
    _, nx, ny, channels = orbitals.shape
    cells = nx * ny
    atoms, k, size = projectors.shape
    part = channels // 16
    y, g = lax.axis_index("pulse"), lax.axis_index("grid")
    quads = slabs // GROUP
    quad = g // GROUP

    def permute(value, target):
        pairs = []
        for p in range(2):
            for s in range(slabs):
                to = target(p, s)
                if to is not None:
                    pairs.append((p * slabs + s, to[0] * slabs + to[1]))
        return lax.ppermute(value, BOTH, pairs)

    def swap_core(value):
        return permute(value, lambda p, s: (p, s ^ 1))

    def shift(value, by):
        return permute(value, lambda p, s: (p, s + by) if 0 <= s + by < slabs else None)

    bundle = jax.ShapeDtypeStruct((5 * channels // 16, cells), F32)
    near, far = pl.pallas_call(
        pack_kernel,
        out_shape=(bundle, bundle),
        in_specs=[VMEM] * 5 + [SMEM],
        out_specs=[VMEM] * 2,
        scratch_shapes=[pltpu.VMEM((cells, channels // 2), F32), pltpu.VMEM((channels // 2, cells), F32)],
        compiler_params=pltpu.CompilerParams(vmem_limit_bytes=8 * 2**20),
        name="pack",
    )(orbitals.reshape(cells, channels), potential.reshape(nx, ny), projectors, couplings.T, sphere_points, atom_count)
    beside = permute(far, lambda p, s: (p, s ^ 2))
    below1, above1 = shift(near, GROUP), shift(near, -GROUP)
    heavy = pl.pallas_call(
        rest_kernel,
        out_shape=jax.ShapeDtypeStruct((32, cells), F32),
        in_specs=[VMEM] * 3,
        out_specs=VMEM,
        compiler_params=pltpu.CompilerParams(vmem_limit_bytes=4 * 2**20),
        name="rest",
    )(projectors, sphere_points, near)
    below2, above2 = shift(beside, GROUP), shift(beside, -GROUP)
    near_mate, pulse_sent = lax.optimization_barrier((swap_core(near), pulse))
    other_pulse = permute(pulse_sent, lambda p, s: (1 - p, s))
    above1, below1, other_pulse = lax.optimization_barrier((above1, below1, other_pulse))
    order = []
    for piece in (below1, below2, near, beside, above1, above2):
        order += [piece, near_mate if piece is near else swap_core(piece)]

    edge = max(slabs // 8, 1)
    shared_heavy = not (edge == 2 and quads >= 4)
    if shared_heavy:
        everywhere = lax.all_gather(heavy, "grid")
        blank = jnp.zeros((HALO - 1,) + heavy.shape, F32)
        padded = jnp.concatenate([blank, everywhere, blank])
        heavies = [lax.dynamic_slice_in_dim(padded, quad * GROUP, SLOTS - 2)]
        stores = SLOTS - 2
    else:
        crowded = (0, 1, slabs - 2, slabs - 1)
        x = (g // 2) % 2
        own = ((quad == 0) & (x == 0)) | ((quad == quads - 1) & (x == 1))
        inner = {1: GROUP, slabs - 2: -GROUP}
        across = permute(heavy, lambda p, s: (p, s ^ 2) if s in crowded else None)
        along = permute(heavy, lambda p, s: (p, s + inner[s]) if s in inner else None)
        over = permute(heavy, lambda p, s: (p, (s + inner[s]) ^ 2) if s in inner else None)
        held = jnp.where(own, heavy, across + along + over)
        heavies = [held, swap_core(held)]
        stores = 2

    outs = pl.pallas_call(
        functools.partial(evolve_kernel, slabs, shared_heavy),
        out_shape=[jax.ShapeDtypeStruct((4 * part, cells), F32)] * 4 + [jax.ShapeDtypeStruct((2 * slabs, 1, 128), F32)],
        in_specs=[SMEM] * 2 + [VMEM] * (12 + len(heavies)),
        out_specs=[VMEM] * 5,
        scratch_shapes=[pltpu.VMEM((SLOTS, 2 * part, cells), F32)]
        + [pltpu.VMEM((SLOTS, 4 * part, cells), F32)] * 3
        + [pltpu.VMEM((SLOTS, 4 * part, cells), BF16)]
        + [pltpu.VMEM((SLOTS, 8 * part, cells), BF16)] * 2
        + [
            pltpu.VMEM((GROUP, 4 * part, cells), F32),
            pltpu.VMEM((SLOTS, 3 * LIGHT * k, cells), BF16),
            pltpu.VMEM((stores, 3 * atoms * k, cells), BF16),
            pltpu.VMEM((SLOTS, 1, cells), F32),
            pltpu.VMEM((SLOTS, 1, 128), F32),
            pltpu.VMEM((2, 2, 4 * part, 3 * LIGHT * k), BF16),
        ],
        compiler_params=pltpu.CompilerParams(vmem_limit_bytes=(28 if not shared_heavy else 40) * 2**20),
        name="evolve",
    )(pulse, other_pulse, *order, *heavies)
    moment = outs[4]
    finals = [
        outs[0],
        permute(outs[1], lambda p, s: (p, s ^ 2)),
        permute(outs[2], lambda p, s: (1 - p, s)),
        permute(outs[3], lambda p, s: (1 - p, s ^ 2)),
    ]
    shares = lax.all_to_all(moment, BOTH, 0, 0)
    *finals, shares = lax.optimization_barrier((*finals, shares))
    pieces = []
    for piece in finals:
        pieces += [piece, swap_core(piece)]
    plane = pl.pallas_call(
        unpack_kernel,
        out_shape=jax.ShapeDtypeStruct((cells, channels), F32),
        in_specs=[VMEM] * 8,
        out_specs=VMEM,
        scratch_shapes=[pltpu.VMEM((channels, cells), F32)] + [pltpu.VMEM((cells, channels // 2), F32)] * 2,
        compiler_params=pltpu.CompilerParams(vmem_limit_bytes=16 * 2**20),
        name="unpack",
    )(*pieces)

    total = jnp.where(y == 0, jnp.sum(shares[:, 0, 0]), jnp.sum(shares[:, 0, 64]))
    dipole = total / (slabs * cells * (channels // 2))
    return plane.reshape(orbitals.shape), dipole.reshape(1)


def solution(mesh):
    placed = (
        P("grid", None, None, None),
        P("grid", None, None),
        P("pulse"),
        P("grid", None, None),
        P("grid", None),
        P("grid", None),
        P("grid"),
    )
    return jax.shard_map(
        functools.partial(local, mesh.shape["grid"]),
        mesh=mesh,
        in_specs=placed,
        out_specs=(P(("pulse", "grid"), None, None, None), P("pulse")),
        check_vma=False,
    )
```
